256 devices in a mesh: seq: 64 (over z, x, core), head: 4 (over y).
Axes of the slice: x: 4, y: 4, z: 8, core: 2. Of those that a mesh axis runs over, the one named last changes fastest.
Arguments:
- query_rows: bfloat16 [32768, 8192], P(('seq', 'head')), may hold values from -6 to 6
- key_rows: bfloat16 [32768, 8192], P(('seq', 'head')), may hold values from -6 to 6
- value_rows: bfloat16 [32768, 8192], P(('seq', 'head')), may hold values from -6 to 6
- destination: int32 [32768], P(('seq', 'head')), may hold values from 0 to 32767, as said below
- doc_lengths: int32 [32], replicated, may hold values from 1 to 2048, 32768 in all
- norm_gain: bfloat16 [8192], P('head'), may hold values from 0.099609375 to 1.8984375
Outputs:
- attended: bfloat16 [32768, 8192], P('seq', 'head')
The draws below stay inside these ranges and needn't reach their ends.
Inputs may be any that keep to these rules, and one draw needn't show every extreme that they name: destination is a permutation of the positions; of the rows of one loader device at most 4 go to one owner's block of 512 positions, and exactly 4 to some owner.
All inputs are finite; a program needn't handle non-finite values.
Results may differ from the reference program's by a relative error of at most 0.0049.
Values may be sent and summed in bfloat16 or wider, within the bound.
No kernel may reach another device: no remote copies, remote signals or barrier semaphores. Data moves between devices by JAX's collectives and lax.ppermute only.
A program may use at most 256 MiB of HBM per device.

```python
import math
import jax
import jax.numpy as jnp
import numpy as np
from jax import lax

HEADS = 64
DH = 128
ROWS_DEV = 512
TOKENS = 32768
CAP = 4
DOCS = 32
MOST = 2048
N_SEQ = 64
N_HEAD = 4


def draw_destination(key, part):
    key = jax.random.fold_in(key, 11)
    owners = N_SEQ
    groups = N_HEAD
    per_loader = ROWS_DEV // N_HEAD
    half_owners = owners // 2
    keys_all = jax.random.split(key, 5)
    picks = jax.random.randint(keys_all[0], (groups, half_owners), 0, CAP + 1)
    picks = picks.at[:, 0].set(CAP)
    pattern = jnp.concatenate([picks, CAP - picks], axis=1).astype(jnp.int32)
    shuffle_one = jax.vmap(lambda sub: jax.random.permutation(sub, owners))
    order_c = shuffle_one(jax.random.split(keys_all[1], groups))
    pattern = jnp.take_along_axis(pattern, order_c, axis=1)
    shift_a = shuffle_one(jax.random.split(keys_all[2], groups))
    shift_b = shuffle_one(jax.random.split(keys_all[3], groups))
    latin = (shift_a[:, :, None] + shift_b[:, None, :]) % owners
    counts = jax.vmap(lambda row, table: row[table])(pattern, latin)
    counts = jnp.transpose(counts, (1, 0, 2)).reshape(owners * groups, owners).astype(jnp.int32)
    offsets = (jnp.cumsum(counts, axis=0) - counts).astype(jnp.int32)
    run_ends = jnp.cumsum(counts, axis=1).astype(jnp.int32)
    run_begins = (run_ends - counts).astype(jnp.int32)
    row_ids = jnp.arange(per_loader).astype(jnp.int32)
    target = jnp.sum((row_ids[None, :, None] >= run_ends[:, None, :]).astype(jnp.int32), axis=2).astype(jnp.int32)
    begin_at = jnp.take_along_axis(run_begins, target, axis=1)
    offset_at = jnp.take_along_axis(offsets, target, axis=1)
    places = target * ROWS_DEV + offset_at + row_ids[None, :] - begin_at
    mixing = jax.vmap(lambda sub: jax.random.permutation(sub, per_loader))(jax.random.split(keys_all[4], owners * groups))
    places = jnp.take_along_axis(places, mixing, axis=1)
    return places.reshape(-1).astype(jnp.int32)


def block_levels(rng, shape, cuts, smallest, top_value):
    level, own = 1.0, jax.random.fold_in(rng, 6)
    for axis_at, shards_of in cuts:
        draws = jnp.exp(jax.random.uniform(jax.random.fold_in(own, axis_at), (shards_of,), jnp.float32, smallest / len(cuts), top_value / len(cuts)))
        level = level * jnp.repeat(draws, shape[axis_at] // shards_of).reshape([-1 if axis == axis_at else 1 for axis in range(len(shape))])
    return level


def split_up(count, total, bound, skew):
    loads = [(1 << 20) // math.isqrt(standing ** skew) + 1 for standing in range(2, count + 1)]
    surplus, given = total - bound - (count - 1), [1] * (count - 1)
    while surplus > 0:
        candidates = [i for i in range(count - 1) if given[i] < bound]
        pool, budget = sum([loads[i] for i in candidates]), surplus
        for i in candidates:
            more = min(bound - given[i], max(1, budget * loads[i] // pool), surplus)
            given[i] = given[i] + more
            surplus = surplus - more
    return np.array([bound] + given)


def uneven_parts(key, amount, total, bound, lean):
    if amount == 2:
        one = jax.random.randint(key, (), max(1, total - bound), min(bound, total - 1) + 1)
        return jnp.stack([one, total - one])
    tallies = jnp.asarray(split_up(amount, total, bound, lean), jnp.int32)
    twos = (amount - 1) // 2
    donor, taker = tallies[1:1 + 2 * twos:2], tallies[2:2 + 2 * twos:2]
    slack = jnp.minimum(donor - 1, bound - taker)
    moved = jax.random.randint(jax.random.fold_in(key, 1), (twos,), 0, 1 << 20) % (slack + 1)
    tallies = tallies.at[1:1 + 2 * twos:2].set(donor - moved).at[2:2 + 2 * twos:2].set(taker + moved)
    return tallies[jax.random.permutation(jax.random.fold_in(key, 2), amount)]


def centred(rng, shape, scale, most, cuts=(), kind=jnp.bfloat16):
    entries = jax.random.normal(rng, shape, jnp.float32) * scale
    if len(cuts) > 0:
        entries = block_levels(rng, shape, cuts, -0.22, 0.18) * entries
    return jnp.clip(entries, min=-most, max=most).astype(kind)


def setup_inputs(seed: int = 0) -> dict:
    splits = jax.random.split(jax.random.key(seed), 7)
    return {
        "query_rows": centred(splits[0], (TOKENS, HEADS * DH), 1.0, 6.0, ((0, 256),)),
        "key_rows": centred(splits[1], (TOKENS, HEADS * DH), 1.0, 6.0, ((0, 256),)),
        "value_rows": centred(splits[2], (TOKENS, HEADS * DH), 1.0, 6.0, ((0, 256),)),
        "destination": draw_destination(jax.random.fold_in(splits[6], 71), 0),
        "doc_lengths": uneven_parts(splits[4], DOCS, TOKENS, MOST, 2).astype(jnp.int32),
        "norm_gain": jnp.clip(1.0 + 0.18 * jax.random.normal(splits[5], (HEADS * DH,), jnp.float32), 0.099609375, 1.8984375).astype(jnp.bfloat16),
    }


def reference(query_rows, key_rows, value_rows, destination, doc_lengths, norm_gain):
    width = HEADS * DH

    def placed(source):
        moved = jnp.zeros_like(source).at[destination].set(source)
        return moved.reshape(N_SEQ, ROWS_DEV, HEADS, DH)
    seq_query = placed(query_rows)
    seq_key = placed(key_rows)
    seq_value = placed(value_rows)
    lengths = doc_lengths.astype(jnp.int32)
    doc_ends = jnp.cumsum(lengths).astype(jnp.int32)
    doc_begins = (doc_ends - lengths).astype(jnp.int32)
    positions = jnp.arange(TOKENS).astype(jnp.int32)
    doc_start = lax.optimization_barrier(jnp.max(jnp.where(doc_begins[None, :] <= positions[:, None], doc_begins[None, :], 0), axis=1)).astype(jnp.int32)
    doc_start = doc_start.reshape(N_SEQ, ROWS_DEV)
    gain_wide = norm_gain.astype(jnp.float32).reshape(HEADS, DH)
    local_index = jnp.arange(ROWS_DEV).astype(jnp.int32)
    begins = (jnp.arange(N_SEQ) * ROWS_DEV).astype(jnp.int32)

    def block(carry_state, inputs):
        query, keyed, valued, starts, begin = inputs
        where_pos = (begin + local_index).astype(jnp.int32)
        allowed = (local_index[None, :] <= local_index[:, None]) & (where_pos[None, :] >= starts[:, None])
        scores = jnp.einsum('qhd,khd->hqk', query.astype(jnp.float32), keyed.astype(jnp.float32))
        weights = jnp.where(allowed[None], scores, 0.0).astype(jnp.bfloat16)
        intra = jnp.einsum('hqk,khd->qhd', weights.astype(jnp.float32), valued.astype(jnp.float32))
        last_start = starts[ROWS_DEV - 1]
        live_keys = (where_pos >= last_start).astype(jnp.bfloat16)
        masked_keys = keyed * live_keys[:, None, None]
        local_state = jnp.einsum('khd,khe->hde', masked_keys.astype(jnp.float32), valued.astype(jnp.float32))
        prior_low = lax.optimization_barrier(carry_state.astype(jnp.bfloat16)).astype(jnp.float32)
        carried = jnp.einsum('qhd,hde->qhe', query.astype(jnp.float32), prior_low)
        use_prior = (starts < begin).astype(jnp.float32)
        combined = intra + use_prior[:, None, None] * carried
        mean_square = lax.optimization_barrier(jnp.mean(combined * combined, axis=-1, keepdims=True))
        result = (combined * lax.rsqrt(mean_square + 1e-06) * gain_wide).astype(jnp.bfloat16)
        new_state = jnp.where(last_start >= begin, local_state, carry_state + local_state)
        return (new_state, result)
    _, outputs = lax.scan(block, jnp.zeros((HEADS, DH, DH), jnp.float32), (seq_query, seq_key, seq_value, doc_start, begins))
    return outputs.reshape(TOKENS, width)
```

```python
import jax
import jax.numpy as jnp
from jax import lax
from jax.experimental import pallas as pl
from jax.experimental.pallas import tpu as pltpu
from jax.sharding import Mesh
from jax.sharding import PartitionSpec as P

DH = 128
OWNED = 512
PLANES = 8
INNER = 8
PLANE_ROWS = INNER * OWNED
WIDE = 2 * DH
ROOM = 592
ROOM_PAD = 640
TILE = 256
TILES = PLANE_ROWS // TILE
BLOCKS = PLANES * INNER
WINDOW = 16
SPAN = 256
SEQ = ("z", "a")
LOCAL = ("head", "a")
VMEM_LIMIT = 56 * 1024 * 1024


def entering(part, axis, combine, identity):
    place = lax.axis_index(axis)
    gathered = jax.tree.map(lambda a: lax.all_gather(a, axis), part)
    state = jax.tree.map(lambda a, e: jnp.zeros_like(a) + jnp.asarray(e, a.dtype), part, identity)

    def one(step, state):
        return combine(
            state, jax.tree.map(lambda a: lax.dynamic_index_in_dim(a, step, 0, False), gathered)
        )

    return lax.fori_loop(0, place, one, state)


def build_slots(tensors, targets, owners, slots, owned):
    owner_index = targets // owned
    onehot = (owner_index[:, None] == jnp.arange(owners, dtype=jnp.int32)[None, :]).astype(
        jnp.int32
    )
    rank_within = jnp.sum((jnp.cumsum(onehot, axis=0) - 1) * onehot, axis=1)
    slot_index = owner_index * slots + rank_within
    buffers = tuple(
        (
            jnp.zeros((owners * slots, tensor.shape[1]), tensor.dtype)
            .at[slot_index]
            .set(tensor)
            .reshape(owners, slots, tensor.shape[1])
            for tensor in tensors
        )
    )
    where_to = (
        jnp.full((owners * slots,), -1, jnp.int32)
        .at[slot_index]
        .set(targets)
        .reshape(owners, slots)
    )
    return (buffers, where_to)


def settle(arrived, where_to, owned, begin):
    local_place = where_to.reshape(-1) - begin
    local_place = jnp.where(where_to.reshape(-1) < 0, owned, local_place).astype(jnp.int32)
    flat = arrived.reshape(-1, arrived.shape[-1])
    return jnp.zeros((owned + 1, flat.shape[1]), flat.dtype).at[local_place].set(flat)[:owned]


def direct(query_rows, key_rows, value_rows, destination, doc_lengths, norm_gain):
    n_seq = lax.axis_size(SEQ)
    n_head = lax.axis_size("head")
    loader_rows = query_rows.shape[0]
    owned = loader_rows * n_head
    narrow = query_rows.shape[1] // n_head
    local_heads = narrow // DH
    capacity = 2 * loader_rows // n_seq
    begin = lax.axis_index(SEQ) * owned
    split_q, split_k, split_v = (
        lax.all_to_all(query_rows, "head", split_axis=1, concat_axis=0, tiled=True),
        lax.all_to_all(key_rows, "head", split_axis=1, concat_axis=0, tiled=True),
        lax.all_to_all(value_rows, "head", split_axis=1, concat_axis=0, tiled=True),
    )
    group_dest = lax.all_gather(destination, "head", axis=0, tiled=True)
    buffers, where_to = build_slots(
        (split_q, split_k, split_v), group_dest, n_seq, n_head * capacity, owned
    )
    got_q, got_k, got_v, got_where = (
        lax.all_to_all(buffers[0], SEQ, split_axis=0, concat_axis=0, tiled=True),
        lax.all_to_all(buffers[1], SEQ, split_axis=0, concat_axis=0, tiled=True),
        lax.all_to_all(buffers[2], SEQ, split_axis=0, concat_axis=0, tiled=True),
        lax.all_to_all(where_to, SEQ, split_axis=0, concat_axis=0, tiled=True),
    )
    seq_query = settle(got_q, got_where, owned, begin).reshape(owned, local_heads, DH)
    seq_key = settle(got_k, got_where, owned, begin).reshape(owned, local_heads, DH)
    seq_value = settle(got_v, got_where, owned, begin).reshape(owned, local_heads, DH)
    doc_ends = jnp.cumsum(doc_lengths)
    doc_begins = doc_ends - doc_lengths
    local_index = jnp.arange(owned, dtype=jnp.int32)
    positions = begin + local_index
    doc_start = jnp.max(
        jnp.where(doc_begins[None, :] <= positions[:, None], doc_begins[None, :], 0), axis=1
    )
    allowed = (local_index[None, :] <= local_index[:, None]) & (
        positions[None, :] >= doc_start[:, None]
    )
    scores = jnp.einsum("qhd,khd->hqk", seq_query, seq_key, preferred_element_type=jnp.float32)
    weights = jnp.where(allowed[None], scores, 0.0).astype(jnp.bfloat16)
    intra = jnp.einsum("hqk,khd->qhd", weights, seq_value, preferred_element_type=jnp.float32)
    last_start = doc_start[owned - 1]
    live_keys = (positions >= last_start).astype(jnp.bfloat16)
    local_state = jnp.einsum(
        "khd,khe->hde",
        seq_key * live_keys[:, None, None],
        seq_value,
        preferred_element_type=jnp.float32,
    )
    restart = jnp.reshape((last_start >= begin).astype(jnp.float32), (1,))

    def combine_states(earlier, later):
        return (later[0] + (1.0 - later[1][0]) * earlier[0], jnp.maximum(earlier[1], later[1]))

    identity = (jnp.zeros_like(local_state), jnp.zeros((1,), jnp.float32))
    prior, _ = entering((local_state, restart), SEQ, combine_states, identity)
    prior_low = prior.astype(jnp.bfloat16)
    carried = jnp.einsum("qhd,hde->qhe", seq_query, prior_low, preferred_element_type=jnp.float32)
    use_prior = (doc_start < begin).astype(jnp.float32)
    combined = intra + use_prior[:, None, None] * carried
    mean_square = jnp.mean(combined * combined, axis=-1, keepdims=True)
    gain_wide = norm_gain.astype(jnp.float32).reshape(local_heads, DH)
    result = combined * lax.rsqrt(mean_square + 1e-06) * gain_wide
    return result.astype(jnp.bfloat16).reshape(owned, narrow)


def in_vmem(count):
    return [pl.BlockSpec(memory_space=pltpu.VMEM)] * count


def in_smem(count):
    return [pl.BlockSpec(memory_space=pltpu.SMEM)] * count


def pack_kernel(starts, slot_ref, rows_ref, *rest):
    out_refs = rest[:PLANES]
    acc, pick, moved = rest[PLANES:]
    acc[...] = jnp.zeros_like(acc)
    step = lax.broadcasted_iota(jnp.int32, (WINDOW, TILE), 0)

    def tile(t, carry):
        slot = slot_ref[pl.ds(t, 1), :]
        for b in range(BLOCKS):
            hit = (step + starts[t * BLOCKS + b]) == slot
            pick[b * WINDOW : (b + 1) * WINDOW, :] = jnp.where(hit, 1.0, 0.0).astype(jnp.bfloat16)
        rows = rows_ref[pl.ds(pl.multiple_of(t * TILE, TILE), TILE), :]
        moved[...] = jnp.dot(pick[...], rows, preferred_element_type=jnp.float32)
        for b in range(BLOCKS):
            place = pl.ds(pl.multiple_of(starts[t * BLOCKS + b], 8), WINDOW)
            acc[place, :] += moved[b * WINDOW : (b + 1) * WINDOW, :]
        return carry

    lax.fori_loop(0, TILES, tile, 0)
    for k in range(PLANES):
        out_refs[k][...] = acc[k * ROOM : (k + 1) * ROOM, :].astype(jnp.bfloat16)


def pack(starts, slots, rows):
    return pl.pallas_call(
        pack_kernel,
        out_shape=[jax.ShapeDtypeStruct((ROOM, WIDE), jnp.bfloat16)] * PLANES,
        in_specs=in_smem(1) + in_vmem(2),
        out_specs=in_vmem(PLANES),
        scratch_shapes=[
            pltpu.VMEM((PLANES * ROOM + WINDOW, WIDE), jnp.float32),
            pltpu.VMEM((BLOCKS * WINDOW, TILE), jnp.bfloat16),
            pltpu.VMEM((BLOCKS * WINDOW, WIDE), jnp.float32),
        ],
        compiler_params=pltpu.CompilerParams(vmem_limit_bytes=VMEM_LIMIT),
        cost_estimate=pl.CostEstimate(
            flops=2 * TILES * BLOCKS * WINDOW * TILE * WIDE, bytes_accessed=6 << 20, transcendentals=0
        ),
        name="pack",
    )(starts, slots, rows)


def fill(pieces, held):
    for k in range(PLANES):
        held[k * ROOM_PAD : k * ROOM_PAD + ROOM, :] = pieces[k][...]
        held[k * ROOM_PAD + ROOM : (k + 1) * ROOM_PAD, :] = jnp.zeros(
            (ROOM_PAD - ROOM, WIDE), jnp.bfloat16
        )


def unpack_block(held, pos_ref, first, b):
    row = lax.broadcasted_iota(jnp.int32, (OWNED, SPAN), 0) + b * OWNED
    total = jnp.zeros((OWNED, WIDE), jnp.float32)
    for k in range(PLANES):
        at = pl.multiple_of(first[k * INNER + b], 128)
        hit = row == pos_ref[k : k + 1, pl.ds(at, SPAN)]
        chosen = jnp.where(hit, 1.0, 0.0).astype(jnp.bfloat16)
        total += jnp.dot(
            chosen, held[pl.ds(k * ROOM_PAD + at, SPAN), :], preferred_element_type=jnp.float32
        )
    return total.astype(jnp.bfloat16)


def state_kernel(first, last_local, pos_ref, *rest):
    key_pieces, value_pieces = rest[:PLANES], rest[PLANES : 2 * PLANES]
    key_out, value_out, prior_out, end_out, held_k, held_v, state = rest[2 * PLANES :]
    fill(key_pieces, held_k)
    fill(value_pieces, held_v)
    state[...] = jnp.zeros_like(state)
    index = lax.broadcasted_iota(jnp.int32, (OWNED, WIDE), 0)

    def block(b, carry):
        at = pl.ds(pl.multiple_of(b * OWNED, OWNED), OWNED)
        keys = unpack_block(held_k, pos_ref, first, b)
        values = unpack_block(held_v, pos_ref, first, b)
        key_out[at, :] = keys
        value_out[at, :] = values
        live = jnp.where(index >= last_local[b], keys, jnp.zeros_like(keys))
        keep = jnp.where(last_local[b] >= 0, 0.0, 1.0)
        for h in range(2):
            cols = slice(h * DH, (h + 1) * DH)
            fresh = lax.dot_general(
                live[:, cols],
                values[:, cols],
                (((0,), (0,)), ((), ())),
                preferred_element_type=jnp.float32,
            )
            before = state[h]
            prior_out[b, h] = before
            state[h] = fresh + keep * before
        return carry

    lax.fori_loop(0, INNER, block, 0)
    end_out[...] = state[...]


def states(first, last_local, pos, key_pieces, value_pieces):
    full = jax.ShapeDtypeStruct((PLANE_ROWS, WIDE), jnp.bfloat16)
    return pl.pallas_call(
        state_kernel,
        out_shape=[
            full,
            full,
            jax.ShapeDtypeStruct((INNER, 2, DH, DH), jnp.float32),
            jax.ShapeDtypeStruct((2, DH, DH), jnp.float32),
        ],
        in_specs=in_smem(2) + in_vmem(1 + 2 * PLANES),
        out_specs=in_vmem(4),
        scratch_shapes=[
            pltpu.VMEM((PLANES * ROOM_PAD, WIDE), jnp.bfloat16),
            pltpu.VMEM((PLANES * ROOM_PAD, WIDE), jnp.bfloat16),
            pltpu.VMEM((2, DH, DH), jnp.float32),
        ],
        compiler_params=pltpu.CompilerParams(vmem_limit_bytes=VMEM_LIMIT),
        cost_estimate=pl.CostEstimate(
            flops=4 * PLANE_ROWS * PLANES * SPAN * WIDE, bytes_accessed=10 << 20, transcendentals=0
        ),
        name="states",
    )(first, last_local, pos, *key_pieces, *value_pieces)


def attend_kernel(first, carries, pos_ref, start_ref, gain_ref, key_ref, value_ref, prior_ref,
                  entry_ref, *rest):
    query_pieces = rest[:PLANES]
    out_ref, held, queries = rest[PLANES:]
    fill(query_pieces, held)
    half = OWNED // 2

    def block(b, carry):
        base = b * OWNED
        queries[...] = unpack_block(held, pos_ref, first, b)
        carried_in = carries[b].astype(jnp.float32)
        for part in range(2):
            width = (part + 1) * half
            rows = pl.ds(pl.multiple_of(base + part * half, half), half)
            starts = start_ref[rows, :]
            row = lax.broadcasted_iota(jnp.int32, (half, width), 0) + part * half
            column = lax.broadcasted_iota(jnp.int32, (half, width), 1)
            allowed = (column <= row) & (column >= starts)
            use_prior = jnp.where(starts < 0, 1.0, 0.0)
            for h in range(2):
                cols = slice(h * DH, (h + 1) * DH)
                query = queries[part * half : (part + 1) * half, cols]
                keys = key_ref[pl.ds(pl.multiple_of(base, OWNED), width), cols]
                values = value_ref[pl.ds(pl.multiple_of(base, OWNED), width), cols]
                scores = lax.dot_general(
                    query, keys, (((1,), (1,)), ((), ())), preferred_element_type=jnp.float32
                )
                weights = jnp.where(allowed, scores, 0.0).astype(jnp.bfloat16)
                intra = jnp.dot(weights, values, preferred_element_type=jnp.float32)
                prior = (prior_ref[b, h] + carried_in * entry_ref[h]).astype(jnp.bfloat16)
                carried = jnp.dot(query, prior, preferred_element_type=jnp.float32)
                combined = intra + use_prior * carried
                square = jnp.mean(combined * combined, axis=-1, keepdims=True)
                result = combined * lax.rsqrt(square + 1e-06) * gain_ref[:, cols]
                out_ref[rows, cols] = result.astype(jnp.bfloat16)
        return carry

    lax.fori_loop(0, INNER, block, 0)


def attend(first, carries, pos, starts, gain, keys, values, prior, entry, query_pieces):
    return pl.pallas_call(
        attend_kernel,
        out_shape=jax.ShapeDtypeStruct((PLANE_ROWS, WIDE), jnp.bfloat16),
        in_specs=in_smem(2) + in_vmem(7 + PLANES),
        out_specs=pl.BlockSpec(memory_space=pltpu.VMEM),
        scratch_shapes=[
            pltpu.VMEM((PLANES * ROOM_PAD, WIDE), jnp.bfloat16),
            pltpu.VMEM((OWNED, WIDE), jnp.bfloat16),
        ],
        compiler_params=pltpu.CompilerParams(vmem_limit_bytes=VMEM_LIMIT),
        cost_estimate=pl.CostEstimate(
            flops=4 * PLANE_ROWS * PLANES * SPAN * WIDE, bytes_accessed=10 << 20, transcendentals=0
        ),
        name="attend",
    )(first, carries, pos, starts, gain, keys, values, prior, entry, *query_pieces)


def spread(rows):
    count = PLANES // 2 * INNER
    parts = jnp.transpose(rows.reshape(rows.shape[0], count, WIDE), (1, 0, 2))
    return lax.all_to_all(parts, LOCAL, split_axis=0, concat_axis=0, tiled=True).reshape(
        PLANE_ROWS, WIDE
    )


def along(pieces):
    moved = [pieces[0]]
    for k in range(1, PLANES):
        pairs = [(i, (i + k) % PLANES) for i in range(PLANES)]
        moved.append(lax.ppermute(pieces[k], "z", pairs))
    return moved


def routing(destination, plane):
    places = lax.all_gather(destination, LOCAL, axis=0, tiled=True)
    owner = places // OWNED
    shift = (owner // INNER - plane) % PLANES
    block = (shift * INNER + owner % INNER).reshape(TILES, TILE)
    same = block[:, :, None] == block[:, None, :]
    at = jnp.arange(TILE)
    within = jnp.sum((same & (at[None, :] < at[:, None])[None]).astype(jnp.int32), axis=2)
    onehot = (block[:, :, None] == jnp.arange(BLOCKS)[None, None, :]).astype(jnp.int32)
    counts = jnp.sum(onehot, axis=1)
    tile_at = jnp.arange(TILES)
    earlier = jnp.sum(
        jnp.where((tile_at[None, :] < tile_at[:, None])[:, :, None], counts[None], 0), axis=1
    )
    totals = jnp.sum(counts, axis=0)
    block_at = jnp.arange(BLOCKS)
    sooner = (block_at[None, :] < block_at[:, None]) & (
        block_at[None, :] // INNER == block_at[:, None] // INNER
    )
    base = jnp.sum(jnp.where(sooner, totals[None, :], 0), axis=1)
    start = earlier + (base + block_at // INNER * ROOM)[None, :]
    slot = within + jnp.sum(onehot * start[:, None, :], axis=2)
    over = jnp.any(jnp.sum(totals.reshape(PLANES, INNER), axis=1) > ROOM).astype(jnp.int32)
    slot = jnp.where(slot < (block // INNER + 1) * ROOM, slot, -1).astype(jnp.int32)
    starts = jnp.minimum(start // 8 * 8, PLANES * ROOM).astype(jnp.int32).reshape(-1)
    flat = slot.reshape(-1)
    table = (
        jnp.full((PLANES * ROOM + 1,), -1, jnp.int32)
        .at[jnp.where(flat < 0, PLANES * ROOM, flat)]
        .set(places % PLANE_ROWS)[: PLANES * ROOM]
        .reshape(PLANES, ROOM)
    )
    pos = jnp.stack(along(list(table)))
    pos = jnp.pad(pos, ((0, 0), (0, ROOM_PAD - ROOM)), constant_values=-1)
    begin = jnp.arange(INNER) * OWNED
    ahead = jnp.sum(
        ((pos[:, None, :] >= 0) & (pos[:, None, :] < begin[None, :, None])).astype(jnp.int32), axis=2
    )
    first = jnp.minimum(ahead // 128 * 128, ROOM_PAD - SPAN).astype(jnp.int32).reshape(-1)
    return slot, starts, pos, first, lax.pmax(over, "z")


def shards(query_rows, key_rows, value_rows, destination, doc_lengths, norm_gain):
    plane = lax.axis_index("z")
    inner = lax.axis_index("a")
    slot, starts, pos, first, over = routing(destination, plane)
    key_pieces = along(pack(starts, slot, spread(key_rows)))
    value_pieces = along(pack(starts, slot, spread(value_rows)))
    query_pieces = along(pack(starts, slot, spread(query_rows)))

    doc_ends = jnp.cumsum(doc_lengths)
    doc_begins = doc_ends - doc_lengths
    positions = plane * PLANE_ROWS + jnp.arange(PLANE_ROWS, dtype=jnp.int32)
    doc_start = jnp.max(
        jnp.where(doc_begins[None, :] <= positions[:, None], doc_begins[None, :], 0), axis=1
    )
    local_start = (doc_start - positions // OWNED * OWNED).astype(jnp.int32)
    last_local = local_start.reshape(INNER, OWNED)[:, OWNED - 1]
    block_at = jnp.arange(INNER)
    carries = jnp.all(
        (block_at[None, :] >= block_at[:, None]) | (last_local[None, :] < 0), axis=1
    ).astype(jnp.int32)

    keys, values, prior, end = states(first, last_local, pos, key_pieces, value_pieces)
    entry = lax.ppermute(end, "z", [(i, i + 1) for i in range(PLANES - 1)])
    gain = lax.dynamic_slice_in_dim(norm_gain.astype(jnp.float32), inner * WIDE, WIDE).reshape(1, WIDE)
    attended = attend(
        first, carries, pos, local_start[:, None], gain, keys, values, prior, entry, query_pieces
    )
    back = lax.all_to_all(
        attended.reshape(INNER, OWNED, WIDE), "a", split_axis=0, concat_axis=0, tiled=True
    )
    result = jnp.transpose(back, (1, 0, 2)).reshape(OWNED, INNER * WIDE)
    return lax.cond(
        over > 0,
        lambda: direct(query_rows, key_rows, value_rows, destination, doc_lengths, norm_gain),
        lambda: result,
    )


def solution(mesh):
    fine = Mesh(mesh.devices.reshape(PLANES, INNER, mesh.shape["head"]), ("z", "a", "head"))
    every = ("z", "a", "head")
    in_specs = (P(every, None), P(every, None), P(every, None), P(every), P(), P("head"))
    return jax.shard_map(
        shards, mesh=fine, in_specs=in_specs, out_specs=P(SEQ, "head"), check_vma=False
    )
```

```python
import jax
import jax.numpy as jnp
from jax import lax
from jax.experimental import pallas as pl
from jax.experimental.pallas import tpu as pltpu
from jax.sharding import Mesh
from jax.sharding import PartitionSpec as P

DH = 128
OWNED = 512
PLANES = 8
INNER = 8
PLANE_ROWS = INNER * OWNED
WIDE = 2 * DH
LOADERS = 32
ROOM = 592
ROOM_PAD = 768
TAIL = 16
TILE = 512
TILES = PLANE_ROWS // TILE
BLOCKS = PLANES * INNER
CELL = 16
STRIP = TILES * CELL
SPAN = 144
CHOICE = PLANES * SPAN
ORDER = (1, 7, 4, 3, 5, 2, 6)
DEPTH = 5
SEQ = ("z", "a")
LOCAL = ("head", "a")
VMEM_LIMIT = 56 * 1024 * 1024


def entering(part, axis, combine, identity):
    place = lax.axis_index(axis)
    gathered = jax.tree.map(lambda a: lax.all_gather(a, axis), part)
    state = jax.tree.map(lambda a, e: jnp.zeros_like(a) + jnp.asarray(e, a.dtype), part, identity)

    def one(step, state):
        return combine(
            state, jax.tree.map(lambda a: lax.dynamic_index_in_dim(a, step, 0, False), gathered)
        )

    return lax.fori_loop(0, place, one, state)


def build_slots(tensors, targets, owners, slots, owned):
    owner_index = targets // owned
    onehot = (owner_index[:, None] == jnp.arange(owners, dtype=jnp.int32)[None, :]).astype(
        jnp.int32
    )
    rank_within = jnp.sum((jnp.cumsum(onehot, axis=0) - 1) * onehot, axis=1)
    slot_index = owner_index * slots + rank_within
    buffers = tuple(
        (
            jnp.zeros((owners * slots, tensor.shape[1]), tensor.dtype)
            .at[slot_index]
            .set(tensor)
            .reshape(owners, slots, tensor.shape[1])
            for tensor in tensors
        )
    )
    where_to = (
        jnp.full((owners * slots,), -1, jnp.int32)
        .at[slot_index]
        .set(targets)
        .reshape(owners, slots)
    )
    return (buffers, where_to)


def settle(arrived, where_to, owned, begin):
    local_place = where_to.reshape(-1) - begin
    local_place = jnp.where(where_to.reshape(-1) < 0, owned, local_place).astype(jnp.int32)
    flat = arrived.reshape(-1, arrived.shape[-1])
    return jnp.zeros((owned + 1, flat.shape[1]), flat.dtype).at[local_place].set(flat)[:owned]


def direct(query_rows, key_rows, value_rows, destination, doc_lengths, norm_gain):
    n_seq = lax.axis_size(SEQ)
    n_head = lax.axis_size("head")
    loader_rows = query_rows.shape[0]
    owned = loader_rows * n_head
    narrow = query_rows.shape[1] // n_head
    local_heads = narrow // DH
    capacity = 2 * loader_rows // n_seq
    begin = lax.axis_index(SEQ) * owned
    split_q, split_k, split_v = (
        lax.all_to_all(query_rows, "head", split_axis=1, concat_axis=0, tiled=True),
        lax.all_to_all(key_rows, "head", split_axis=1, concat_axis=0, tiled=True),
        lax.all_to_all(value_rows, "head", split_axis=1, concat_axis=0, tiled=True),
    )
    group_dest = lax.all_gather(destination, "head", axis=0, tiled=True)
    buffers, where_to = build_slots(
        (split_q, split_k, split_v), group_dest, n_seq, n_head * capacity, owned
    )
    got_q, got_k, got_v, got_where = (
        lax.all_to_all(buffers[0], SEQ, split_axis=0, concat_axis=0, tiled=True),
        lax.all_to_all(buffers[1], SEQ, split_axis=0, concat_axis=0, tiled=True),
        lax.all_to_all(buffers[2], SEQ, split_axis=0, concat_axis=0, tiled=True),
        lax.all_to_all(where_to, SEQ, split_axis=0, concat_axis=0, tiled=True),
    )
    seq_query = settle(got_q, got_where, owned, begin).reshape(owned, local_heads, DH)
    seq_key = settle(got_k, got_where, owned, begin).reshape(owned, local_heads, DH)
    seq_value = settle(got_v, got_where, owned, begin).reshape(owned, local_heads, DH)
    doc_ends = jnp.cumsum(doc_lengths)
    doc_begins = doc_ends - doc_lengths
    local_index = jnp.arange(owned, dtype=jnp.int32)
    positions = begin + local_index
    doc_start = jnp.max(
        jnp.where(doc_begins[None, :] <= positions[:, None], doc_begins[None, :], 0), axis=1
    )
    allowed = (local_index[None, :] <= local_index[:, None]) & (
        positions[None, :] >= doc_start[:, None]
    )
    scores = jnp.einsum("qhd,khd->hqk", seq_query, seq_key, preferred_element_type=jnp.float32)
    weights = jnp.where(allowed[None], scores, 0.0).astype(jnp.bfloat16)
    intra = jnp.einsum("hqk,khd->qhd", weights, seq_value, preferred_element_type=jnp.float32)
    last_start = doc_start[owned - 1]
    live_keys = (positions >= last_start).astype(jnp.bfloat16)
    local_state = jnp.einsum(
        "khd,khe->hde",
        seq_key * live_keys[:, None, None],
        seq_value,
        preferred_element_type=jnp.float32,
    )
    restart = jnp.reshape((last_start >= begin).astype(jnp.float32), (1,))

    def combine_states(earlier, later):
        return (later[0] + (1.0 - later[1][0]) * earlier[0], jnp.maximum(earlier[1], later[1]))

    identity = (jnp.zeros_like(local_state), jnp.zeros((1,), jnp.float32))
    prior, _ = entering((local_state, restart), SEQ, combine_states, identity)
    prior_low = prior.astype(jnp.bfloat16)
    carried = jnp.einsum("qhd,hde->qhe", seq_query, prior_low, preferred_element_type=jnp.float32)
    use_prior = (doc_start < begin).astype(jnp.float32)
    combined = intra + use_prior[:, None, None] * carried
    mean_square = jnp.mean(combined * combined, axis=-1, keepdims=True)
    gain_wide = norm_gain.astype(jnp.float32).reshape(local_heads, DH)
    result = combined * lax.rsqrt(mean_square + 1e-06) * gain_wide
    return result.astype(jnp.bfloat16).reshape(owned, narrow)


def whole(*shape):
    return pl.BlockSpec(shape, lambda *_: (0,) * len(shape))


def in_smem():
    return pl.BlockSpec(memory_space=pltpu.SMEM)


def anywhere(count):
    return [pl.BlockSpec(memory_space=pl.ANY)] * count


def params():
    return pltpu.CompilerParams(vmem_limit_bytes=VMEM_LIMIT)


def cost(flops, size):
    return pl.CostEstimate(flops=flops, bytes_accessed=size, transcendentals=0)


def split_kernel(in_ref, *rest):
    for i in range(LOADERS):
        rest[-1][i] = in_ref[:, i * WIDE : (i + 1) * WIDE]


def split(rows, after=()):
    count = rows.shape[0]
    return pl.pallas_call(
        split_kernel,
        out_shape=jax.ShapeDtypeStruct((LOADERS, count, WIDE), rows.dtype),
        in_specs=[pl.BlockSpec(memory_space=pltpu.VMEM)] + anywhere(len(after)),
        out_specs=pl.BlockSpec(memory_space=pltpu.VMEM),
        compiler_params=params(),
        cost_estimate=cost(0, 4 << 20),
        name="split",
    )(rows, *after)


def pack_kernel(tailed, firsts, *refs):
    if tailed:
        over, cell_ref, strip_ref, label_ref, rows_ref = refs[:5]
        cells, slots, label_cells, label_slots = refs[-4:]
        out_refs = refs[-4 - PLANES : -4]
        label_slots[...] = jnp.zeros_like(label_slots)
    else:
        cell_ref, strip_ref, rows_ref = refs[:3]
        cells, slots = refs[-2:]
        out_refs = refs[-2 - PLANES : -2]
    slots[...] = jnp.zeros_like(slots)
    cell = lax.broadcasted_iota(jnp.int32, (BLOCKS * CELL, TILE), 0)
    for t in range(TILES):
        pick = jnp.where(cell == cell_ref[t : t + 1, :], 1.0, 0.0).astype(jnp.bfloat16)
        sorted_rows = jnp.dot(
            pick, rows_ref[t * TILE : (t + 1) * TILE, :], preferred_element_type=jnp.float32
        ).astype(jnp.bfloat16)
        for b in range(BLOCKS):
            at = b * STRIP + t * CELL
            cells[at : at + CELL, :] = sorted_rows[b * CELL : (b + 1) * CELL, :]
        if tailed:
            sorted_labels = lax.dot_general(
                pick, label_ref[t], (((1,), (1,)), ((), ())), preferred_element_type=jnp.float32
            ).astype(jnp.bfloat16)
            for b in range(BLOCKS):
                at = b * STRIP + t * CELL
                label_cells[at : at + CELL, :] = sorted_labels[b * CELL : (b + 1) * CELL, :]
    step = lax.broadcasted_iota(jnp.int32, (SPAN, STRIP), 0)
    for b in range(BLOCKS):
        pick = jnp.where(step == strip_ref[b : b + 1, :], 1.0, 0.0).astype(jnp.bfloat16)
        strip = slice(b * STRIP, (b + 1) * STRIP)
        dense = jnp.dot(pick, cells[strip, :], preferred_element_type=jnp.float32).astype(
            jnp.bfloat16
        )
        first = pl.multiple_of(firsts[b], CELL)
        slots[pl.ds(first, CELL), :] += dense[:CELL, :]
        slots[pl.ds(first + CELL, SPAN - CELL), :] = dense[CELL:, :]
        if tailed:
            dense = jnp.dot(pick, label_cells[strip, :], preferred_element_type=jnp.float32)
            label_slots[pl.ds(first, CELL), :] += dense[:CELL, :]
            label_slots[pl.ds(first + CELL, SPAN - CELL), :] = dense[CELL:, :]
    for k in range(PLANES):
        out_refs[k][:ROOM, :] = slots[k * ROOM : (k + 1) * ROOM, :]
        if tailed:
            line = jnp.transpose(label_slots[k * ROOM : k * ROOM + ROOM_PAD, :])[:2, :]
            rows = [line[:, i * WIDE : (i + 1) * WIDE] for i in range(ROOM_PAD // WIDE)]
            flag = jnp.full((TAIL - 2 * len(rows), WIDE), over[0], jnp.int32).astype(jnp.float32)
            out_refs[k][ROOM:, :] = jnp.concatenate(rows + [flag], axis=0).astype(jnp.bfloat16)


def pack(firsts, cell, strip, rows, labels=None, over=None, after=()):
    tailed = labels is not None
    height = ROOM + TAIL if tailed else ROOM
    label_scratch = [
        pltpu.VMEM((BLOCKS * STRIP, DH), jnp.bfloat16),
        pltpu.VMEM((PLANES * ROOM + ROOM_PAD - ROOM + CELL, DH), jnp.float32),
    ]
    return pl.pallas_call(
        lambda *refs: pack_kernel(tailed, *refs),
        out_shape=[jax.ShapeDtypeStruct((height, WIDE), jnp.bfloat16)] * PLANES,
        in_specs=[in_smem()] * (2 if tailed else 1)
        + [pl.BlockSpec(memory_space=pltpu.VMEM)] * (4 if tailed else 3)
        + anywhere(len(after)),
        out_specs=[pl.BlockSpec(memory_space=pltpu.VMEM)] * PLANES,
        scratch_shapes=[
            pltpu.VMEM((BLOCKS * STRIP, WIDE), jnp.bfloat16),
            pltpu.VMEM((PLANES * ROOM + SPAN, WIDE), jnp.bfloat16),
        ]
        + (label_scratch if tailed else []),
        compiler_params=params(),
        cost_estimate=cost(2 * PLANE_ROWS * BLOCKS * CELL * WIDE, 16 << 20),
        name="pack",
    )(*((firsts, over, cell, strip, labels, rows) if tailed else (firsts, cell, strip, rows)), *after)


def gather_near(pieces, first, b, near, cols):
    for k in range(PLANES):
        from_row = pl.ds(pl.multiple_of(first[k * INNER + b], CELL), SPAN)
        near[k * SPAN : (k + 1) * SPAN, cols] = pieces[k][from_row, :]


def state_kernel(first, last_local, pos_ref, start_ref, *rest):
    key_pieces, value_pieces = rest[:PLANES], rest[PLANES : 2 * PLANES]
    choice_ref, mask_ref, key_out, value_out, prior_out, end_out, near, state = rest[2 * PLANES :]
    b = pl.program_id(0)

    @pl.when(b == 0)
    def _():
        state[...] = jnp.zeros_like(state)

    lane = lax.broadcasted_iota(jnp.int32, (PLANES, CHOICE), 1)
    line = jnp.full((1, CHOICE), -1, jnp.int32)
    for k in range(PLANES):
        shift = (k * SPAN - first[k * INNER + b] + CHOICE) % CHOICE
        rolled = pltpu.roll(pos_ref[...], shift, 1)
        inside = (lane >= k * SPAN) & (lane < (k + 1) * SPAN)
        line = jnp.where(inside, rolled, line)[k : k + 1, :] if k == 0 else jnp.where(
            inside[:1], rolled[k : k + 1, :], line
        )
    row = lax.broadcasted_iota(jnp.int32, (OWNED, CHOICE), 0)
    choice_ref[0] = jnp.where(row == line - b * OWNED, 1.0, 0.0).astype(jnp.bfloat16)
    gather_near(key_pieces, first, b, near, slice(0, WIDE))
    gather_near(value_pieces, first, b, near, slice(WIDE, 2 * WIDE))
    both = jnp.dot(choice_ref[0], near[...], preferred_element_type=jnp.float32).astype(jnp.bfloat16)
    keys, values = both[:, :WIDE], both[:, WIDE:]
    key_out[...] = keys
    value_out[...] = values
    index = lax.broadcasted_iota(jnp.int32, (OWNED, WIDE), 0)
    live = jnp.where(index >= last_local[b], keys, jnp.zeros_like(keys))
    keep = jnp.where(last_local[b] >= 0, 0.0, 1.0)
    for h in range(2):
        cols = slice(h * DH, (h + 1) * DH)
        fresh = lax.dot_general(
            live[:, cols],
            values[:, cols],
            (((0,), (0,)), ((), ())),
            preferred_element_type=jnp.float32,
        )
        before = state[h]
        prior_out[0, h] = before
        state[h] = fresh + keep * before
    end_out[...] = state[...]
    row = lax.broadcasted_iota(jnp.int32, (OWNED, OWNED), 0)
    column = lax.broadcasted_iota(jnp.int32, (OWNED, OWNED), 1)
    allowed = (column <= row) & (column >= start_ref[...])
    mask_ref[0] = jnp.where(allowed, 1.0, 0.0).astype(jnp.bfloat16)


def states(first, last_local, pos, starts, key_pieces, value_pieces):
    full = jax.ShapeDtypeStruct((PLANE_ROWS, WIDE), jnp.bfloat16)
    return pl.pallas_call(
        state_kernel,
        grid=(INNER,),
        out_shape=[
            jax.ShapeDtypeStruct((INNER, OWNED, CHOICE), jnp.bfloat16),
            jax.ShapeDtypeStruct((INNER, OWNED, OWNED), jnp.bfloat16),
            full,
            full,
            jax.ShapeDtypeStruct((INNER, 2, DH, DH), jnp.float32),
            jax.ShapeDtypeStruct((2, DH, DH), jnp.float32),
        ],
        in_specs=[
            in_smem(),
            in_smem(),
            whole(PLANES, CHOICE),
            pl.BlockSpec((OWNED, 1), lambda i: (i, 0)),
        ]
        + [whole(ROOM, WIDE)] * PLANES
        + [whole(ROOM + TAIL, WIDE)] * PLANES,
        out_specs=[
            pl.BlockSpec((1, OWNED, CHOICE), lambda i: (i, 0, 0)),
            pl.BlockSpec((1, OWNED, OWNED), lambda i: (i, 0, 0)),
            pl.BlockSpec((OWNED, WIDE), lambda i: (i, 0)),
            pl.BlockSpec((OWNED, WIDE), lambda i: (i, 0)),
            pl.BlockSpec((1, 2, DH, DH), lambda i: (i, 0, 0, 0)),
            whole(2, DH, DH),
        ],
        scratch_shapes=[
            pltpu.VMEM((CHOICE, 2 * WIDE), jnp.bfloat16),
            pltpu.VMEM((2, DH, DH), jnp.float32),
        ],
        compiler_params=params(),
        cost_estimate=cost(4 * PLANE_ROWS * CHOICE * WIDE, 30 << 20),
        name="states",
    )(first, last_local, pos, starts, *key_pieces, *value_pieces)


def attend_kernel(first, carries, choice_ref, mask_ref, use_ref, gain_ref, key_ref, value_ref,
                  prior_ref, entry_ref, *rest):
    query_pieces = rest[:PLANES]
    out_ref, near = rest[PLANES:]
    half = OWNED // 2
    b = pl.program_id(0)
    gather_near(query_pieces, first, b, near, slice(0, WIDE))
    queries = jnp.dot(
        choice_ref[0], near[...], preferred_element_type=jnp.float32
    ).astype(jnp.bfloat16)
    carried_in = carries[b].astype(jnp.float32)
    for h in range(2):
        cols = slice(h * DH, (h + 1) * DH)
        prior = (prior_ref[0, h] + carried_in * entry_ref[h]).astype(jnp.bfloat16)
        for part in range(2):
            width = (part + 1) * half
            rows = slice(part * half, (part + 1) * half)
            query = queries[rows, cols]
            scores = lax.dot_general(
                query, key_ref[:width, cols], (((1,), (1,)), ((), ())),
                preferred_element_type=jnp.float32,
            )
            weights = scores.astype(jnp.bfloat16) * mask_ref[0, rows, :width]
            combined = jnp.dot(
                weights, value_ref[:width, cols], preferred_element_type=jnp.float32
            ) + jnp.dot(query * use_ref[rows, :], prior, preferred_element_type=jnp.float32)
            square = jnp.mean(combined * combined, axis=-1, keepdims=True)
            result = combined * lax.rsqrt(square + 1e-06) * gain_ref[:, cols]
            out_ref[0, rows, cols] = result.astype(jnp.bfloat16)


def attend(first, carries, choice, mask, use, gain, keys, values, prior, entry, query_pieces):
    return pl.pallas_call(
        attend_kernel,
        grid=(INNER,),
        out_shape=jax.ShapeDtypeStruct((INNER, OWNED, WIDE), jnp.bfloat16),
        in_specs=[
            in_smem(),
            in_smem(),
            pl.BlockSpec((1, OWNED, CHOICE), lambda i: (i, 0, 0)),
            pl.BlockSpec((1, OWNED, OWNED), lambda i: (i, 0, 0)),
            pl.BlockSpec((OWNED, DH), lambda i: (i, 0)),
            whole(1, WIDE),
            pl.BlockSpec((OWNED, WIDE), lambda i: (i, 0)),
            pl.BlockSpec((OWNED, WIDE), lambda i: (i, 0)),
            pl.BlockSpec((1, 2, DH, DH), lambda i: (i, 0, 0, 0)),
            whole(2, DH, DH),
        ]
        + [whole(ROOM, WIDE)] * PLANES,
        out_specs=pl.BlockSpec((1, OWNED, WIDE), lambda i: (i, 0, 0)),
        scratch_shapes=[pltpu.VMEM((CHOICE, WIDE), jnp.bfloat16)],
        compiler_params=params(),
        cost_estimate=cost(4 * PLANE_ROWS * CHOICE * WIDE, 30 << 20),
        name="attend",
    )(first, carries, choice, mask, use, gain, keys, values, prior, entry, *query_pieces)


def join_kernel(in_ref, out_ref):
    for i in range(INNER):
        out_ref[:, i * WIDE : (i + 1) * WIDE] = in_ref[i]


def join(parts):
    return pl.pallas_call(
        join_kernel,
        out_shape=jax.ShapeDtypeStruct((OWNED, INNER * WIDE), jnp.bfloat16),
        in_specs=[pl.BlockSpec(memory_space=pltpu.VMEM)],
        out_specs=pl.BlockSpec(memory_space=pltpu.VMEM),
        compiler_params=params(),
        cost_estimate=cost(0, 4 << 20),
        name="join",
    )(parts)


def spread(parts):
    return lax.all_to_all(parts, LOCAL, split_axis=0, concat_axis=0, tiled=True).reshape(
        PLANE_ROWS, WIDE
    )


class Lane:
    def __init__(self):
        self.arrived = []

    def send(self, piece, k):
        if len(self.arrived) >= DEPTH:
            piece, _ = lax.optimization_barrier((piece, self.arrived[-DEPTH]))
        pairs = [(i, (i + k) % PLANES) for i in range(PLANES)]
        moved = lax.ppermute(piece, "z", pairs)
        self.arrived.append(moved)
        return moved

    def exchange(self, pieces, after={}):
        moved = {0: pieces[0]}
        for i, k in enumerate(ORDER):
            piece = pieces[k]
            if i in after:
                piece, _ = lax.optimization_barrier((piece, after[i]))
            moved[k] = self.send(piece, k)
        return [moved[k] for k in range(PLANES)]


def slotting(places, plane):
    owner = places // OWNED
    shift = (owner // INNER - plane) % PLANES
    block = (shift * INNER + owner % INNER).reshape(TILES, TILE)
    same = block[:, :, None] == block[:, None, :]
    at = jnp.arange(TILE)
    within = jnp.sum((same & (at[None, :] < at[:, None])[None]).astype(jnp.int32), axis=2)
    onehot = (block[:, :, None] == jnp.arange(BLOCKS)[None, None, :]).astype(jnp.int32)
    counts = jnp.sum(onehot, axis=1)
    tile_at = jnp.arange(TILES)
    earlier = jnp.sum(
        jnp.where((tile_at[None, :] < tile_at[:, None])[:, :, None], counts[None], 0), axis=1
    )
    totals = jnp.sum(counts, axis=0)
    block_at = jnp.arange(BLOCKS)
    sooner = (block_at[None, :] < block_at[:, None]) & (
        block_at[None, :] // INNER == block_at[:, None] // INNER
    )
    base = jnp.sum(jnp.where(sooner, totals[None, :], 0), axis=1)
    start = earlier + (base + block_at // INNER * ROOM)[None, :]
    firsts = jnp.minimum(start[0] // CELL * CELL, PLANES * ROOM).astype(jnp.int32)
    inside = jnp.arange(CELL)
    strip = jnp.where(
        inside[None, None, :] < counts.T[:, :, None],
        (start - firsts[None, :]).T[:, :, None] + inside[None, None, :],
        -1,
    ).reshape(BLOCKS, STRIP)
    cell = block * CELL + within
    over = jnp.any(jnp.sum(totals.reshape(PLANES, INNER), axis=1) > ROOM).astype(jnp.int32)
    return cell.astype(jnp.int32), strip.astype(jnp.int32), firsts, over.reshape(1)


def label(places):
    value = (places % PLANE_ROWS + 1).reshape(TILES, 1, TILE)
    digit = jnp.arange(DH)[None, :, None]
    return jnp.where(
        digit == 0, value // 64, jnp.where(digit == 1, value % 64, 0)
    ).astype(jnp.bfloat16)


def read_labels(tails):
    line = tails[:, : 2 * (ROOM_PAD // WIDE), :].reshape(PLANES, ROOM_PAD // WIDE, 2, WIDE)
    line = jnp.transpose(line, (0, 2, 1, 3)).reshape(PLANES, 2, ROOM_PAD).astype(jnp.int32)
    pos = (line[:, 0, :] * 64 + line[:, 1, :] - 1)[:, :ROOM]
    over = jnp.max(tails[:, TAIL - 1, 0]).astype(jnp.int32)
    begin = jnp.arange(INNER) * OWNED
    ahead = jnp.sum(
        ((pos[:, None, :] >= 0) & (pos[:, None, :] < begin[None, :, None])).astype(jnp.int32), axis=2
    )
    first = jnp.minimum(ahead // CELL * CELL, ROOM - SPAN).astype(jnp.int32).reshape(-1)
    pos = jnp.pad(pos, ((0, 0), (0, CHOICE - ROOM)), constant_values=-1)
    return pos, first, over


def shards(query_rows, key_rows, value_rows, destination, doc_lengths, norm_gain):
    plane = lax.axis_index("z")
    inner = lax.axis_index("a")
    count = destination.shape[0]
    places = lax.all_to_all(
        jnp.broadcast_to(destination[None], (LOADERS, count)), LOCAL, split_axis=0, concat_axis=0, tiled=True
    ).reshape(-1)
    cell, strip, firsts, over = slotting(places, plane)
    key_parts, _ = lax.optimization_barrier((split(key_rows), places))
    key_rows_there = spread(key_parts)
    value_rows_there = spread(split(value_rows, (cell, strip)))
    lane = Lane()
    key_packed = pack(firsts, cell, strip, key_rows_there)
    key_pieces = lane.exchange(key_packed)
    value_packed = pack(firsts, cell, strip, value_rows_there, label(places), over)
    query_rows_there = spread(split(query_rows, (value_packed[0], *key_pieces[1:])))
    value_pieces = lane.exchange(value_packed)
    query_packed = pack(firsts, cell, strip, query_rows_there, after=value_pieces[1:])
    query_pieces = lane.exchange(query_packed)
    doc_lengths_then, _ = lax.optimization_barrier((doc_lengths, key_pieces[1]))
    value_pieces[0], _ = lax.optimization_barrier((value_pieces[0], lane.arrived[15]))
    pos, first, any_over = read_labels(jnp.stack([piece[ROOM:] for piece in value_pieces]))

    doc_ends = jnp.cumsum(doc_lengths_then)
    doc_begins = doc_ends - doc_lengths_then
    positions = plane * PLANE_ROWS + jnp.arange(PLANE_ROWS, dtype=jnp.int32)
    doc_start = jnp.max(
        jnp.where(doc_begins[None, :] <= positions[:, None], doc_begins[None, :], 0), axis=1
    )
    local_start = (doc_start - positions // OWNED * OWNED).astype(jnp.int32)
    last_local = local_start.reshape(INNER, OWNED)[:, OWNED - 1]
    block_at = jnp.arange(INNER)
    carries = jnp.all(
        (block_at[None, :] >= block_at[:, None]) | (last_local[None, :] < 0), axis=1
    ).astype(jnp.int32)
    use = jnp.broadcast_to((local_start < 0).astype(jnp.bfloat16)[:, None], (PLANE_ROWS, DH))

    choice, mask, keys, values, prior, end = states(
        first, last_local, pos, local_start[:, None], key_pieces, value_pieces
    )
    entry = lax.ppermute(end, "z", [(i, i + 1) for i in range(PLANES - 1)])
    gain = lax.dynamic_slice_in_dim(norm_gain.astype(jnp.float32), inner * WIDE, WIDE).reshape(1, WIDE)
    attended = attend(
        first, carries, choice, mask, use, gain, keys, values, prior, entry, query_pieces
    )
    back = lax.all_to_all(attended, "a", split_axis=0, concat_axis=0, tiled=True)
    return lax.cond(
        any_over > 0,
        lambda: direct(query_rows, key_rows, value_rows, destination, doc_lengths, norm_gain),
        lambda: join(back),
    )


def solution(mesh):
    fine = Mesh(mesh.devices.reshape(PLANES, INNER, mesh.shape["head"]), ("z", "a", "head"))
    every = ("z", "a", "head")
    in_specs = (P(every, None), P(every, None), P(every, None), P(every), P(), P("head"))
    return jax.shard_map(
        shards, mesh=fine, in_specs=in_specs, out_specs=P(SEQ, "head"), check_vma=False
    )
```

```python
import jax
import jax.numpy as jnp
from jax import lax
from jax.experimental import pallas as pl
from jax.experimental.pallas import tpu as pltpu
from jax.sharding import Mesh
from jax.sharding import PartitionSpec as P

DH = 128
OWNED = 512
PLANES = 8
INNER = 8
PLANE_ROWS = INNER * OWNED
WIDE = 2 * DH
LOADERS = 32
ROOM = 592
ROOM_PAD = 768
TAIL = 16
TILE = 512
TILES = PLANE_ROWS // TILE
BLOCKS = PLANES * INNER
CELL = 16
STRIP = TILES * CELL
SPAN = 144
CHOICE = PLANES * SPAN
ORDER = (3, 5, 1, 7, 4, 2, 6)
AHEAD = {2: 1, 6: 7}
SEQ = ("z", "a")
LOCAL = ("head", "a")
VMEM_LIMIT = 56 * 1024 * 1024


def entering(part, axis, combine, identity):
    place = lax.axis_index(axis)
    gathered = jax.tree.map(lambda a: lax.all_gather(a, axis), part)
    state = jax.tree.map(lambda a, e: jnp.zeros_like(a) + jnp.asarray(e, a.dtype), part, identity)

    def one(step, state):
        return combine(
            state, jax.tree.map(lambda a: lax.dynamic_index_in_dim(a, step, 0, False), gathered)
        )

    return lax.fori_loop(0, place, one, state)


def build_slots(tensors, targets, owners, slots, owned):
    owner_index = targets // owned
    onehot = (owner_index[:, None] == jnp.arange(owners, dtype=jnp.int32)[None, :]).astype(
        jnp.int32
    )
    rank_within = jnp.sum((jnp.cumsum(onehot, axis=0) - 1) * onehot, axis=1)
    slot_index = owner_index * slots + rank_within
    buffers = tuple(
        (
            jnp.zeros((owners * slots, tensor.shape[1]), tensor.dtype)
            .at[slot_index]
            .set(tensor)
            .reshape(owners, slots, tensor.shape[1])
            for tensor in tensors
        )
    )
    where_to = (
        jnp.full((owners * slots,), -1, jnp.int32)
        .at[slot_index]
        .set(targets)
        .reshape(owners, slots)
    )
    return (buffers, where_to)


def settle(arrived, where_to, owned, begin):
    local_place = where_to.reshape(-1) - begin
    local_place = jnp.where(where_to.reshape(-1) < 0, owned, local_place).astype(jnp.int32)
    flat = arrived.reshape(-1, arrived.shape[-1])
    return jnp.zeros((owned + 1, flat.shape[1]), flat.dtype).at[local_place].set(flat)[:owned]


def direct(query_rows, key_rows, value_rows, destination, doc_lengths, norm_gain):
    n_seq = lax.axis_size(SEQ)
    n_head = lax.axis_size("head")
    loader_rows = query_rows.shape[0]
    owned = loader_rows * n_head
    narrow = query_rows.shape[1] // n_head
    local_heads = narrow // DH
    capacity = 2 * loader_rows // n_seq
    begin = lax.axis_index(SEQ) * owned
    split_q, split_k, split_v = (
        lax.all_to_all(query_rows, "head", split_axis=1, concat_axis=0, tiled=True),
        lax.all_to_all(key_rows, "head", split_axis=1, concat_axis=0, tiled=True),
        lax.all_to_all(value_rows, "head", split_axis=1, concat_axis=0, tiled=True),
    )
    group_dest = lax.all_gather(destination, "head", axis=0, tiled=True)
    buffers, where_to = build_slots(
        (split_q, split_k, split_v), group_dest, n_seq, n_head * capacity, owned
    )
    got_q, got_k, got_v, got_where = (
        lax.all_to_all(buffers[0], SEQ, split_axis=0, concat_axis=0, tiled=True),
        lax.all_to_all(buffers[1], SEQ, split_axis=0, concat_axis=0, tiled=True),
        lax.all_to_all(buffers[2], SEQ, split_axis=0, concat_axis=0, tiled=True),
        lax.all_to_all(where_to, SEQ, split_axis=0, concat_axis=0, tiled=True),
    )
    seq_query = settle(got_q, got_where, owned, begin).reshape(owned, local_heads, DH)
    seq_key = settle(got_k, got_where, owned, begin).reshape(owned, local_heads, DH)
    seq_value = settle(got_v, got_where, owned, begin).reshape(owned, local_heads, DH)
    doc_ends = jnp.cumsum(doc_lengths)
    doc_begins = doc_ends - doc_lengths
    local_index = jnp.arange(owned, dtype=jnp.int32)
    positions = begin + local_index
    doc_start = jnp.max(
        jnp.where(doc_begins[None, :] <= positions[:, None], doc_begins[None, :], 0), axis=1
    )
    allowed = (local_index[None, :] <= local_index[:, None]) & (
        positions[None, :] >= doc_start[:, None]
    )
    scores = jnp.einsum("qhd,khd->hqk", seq_query, seq_key, preferred_element_type=jnp.float32)
    weights = jnp.where(allowed[None], scores, 0.0).astype(jnp.bfloat16)
    intra = jnp.einsum("hqk,khd->qhd", weights, seq_value, preferred_element_type=jnp.float32)
    last_start = doc_start[owned - 1]
    live_keys = (positions >= last_start).astype(jnp.bfloat16)
    local_state = jnp.einsum(
        "khd,khe->hde",
        seq_key * live_keys[:, None, None],
        seq_value,
        preferred_element_type=jnp.float32,
    )
    restart = jnp.reshape((last_start >= begin).astype(jnp.float32), (1,))

    def combine_states(earlier, later):
        return (later[0] + (1.0 - later[1][0]) * earlier[0], jnp.maximum(earlier[1], later[1]))

    identity = (jnp.zeros_like(local_state), jnp.zeros((1,), jnp.float32))
    prior, _ = entering((local_state, restart), SEQ, combine_states, identity)
    prior_low = prior.astype(jnp.bfloat16)
    carried = jnp.einsum("qhd,hde->qhe", seq_query, prior_low, preferred_element_type=jnp.float32)
    use_prior = (doc_start < begin).astype(jnp.float32)
    combined = intra + use_prior[:, None, None] * carried
    mean_square = jnp.mean(combined * combined, axis=-1, keepdims=True)
    gain_wide = norm_gain.astype(jnp.float32).reshape(local_heads, DH)
    result = combined * lax.rsqrt(mean_square + 1e-06) * gain_wide
    return result.astype(jnp.bfloat16).reshape(owned, narrow)


def whole(*shape):
    return pl.BlockSpec(shape, lambda *_: (0,) * len(shape))


def in_smem():
    return pl.BlockSpec(memory_space=pltpu.SMEM)


def anywhere(count):
    return [pl.BlockSpec(memory_space=pl.ANY)] * count


def params():
    return pltpu.CompilerParams(vmem_limit_bytes=VMEM_LIMIT)


def cost(flops, size):
    return pl.CostEstimate(flops=flops, bytes_accessed=size, transcendentals=0)


def split_kernel(labelled, in_ref, *rest):
    out_ref = rest[-1]
    count = in_ref.shape[0]
    for i in range(LOADERS):
        out_ref[i, :count, :] = in_ref[:, i * WIDE : (i + 1) * WIDE]
        if labelled:
            out_ref[i, count:, :] = rest[0][...]


def split(rows, after=(), spare=None):
    labelled = spare is not None
    count = rows.shape[0] + (spare.shape[0] if labelled else 0)
    return pl.pallas_call(
        lambda *refs: split_kernel(labelled, *refs),
        out_shape=jax.ShapeDtypeStruct((LOADERS, count, WIDE), rows.dtype),
        in_specs=[pl.BlockSpec(memory_space=pltpu.VMEM)] * (2 if labelled else 1)
        + anywhere(len(after)),
        out_specs=pl.BlockSpec(memory_space=pltpu.VMEM),
        compiler_params=params(),
        cost_estimate=cost(0, 4 << 20),
        name="split",
    )(rows, *((spare,) if labelled else ()), *after)


def pack_kernel(tailed, firsts, *refs):
    if tailed:
        over, cell_ref, strip_ref, label_ref, rows_ref = refs[:5]
        cells, slots, label_cells, label_slots = refs[-4:]
        out_refs = refs[-4 - PLANES : -4]
        label_slots[...] = jnp.zeros_like(label_slots)
    else:
        cell_ref, strip_ref, rows_ref = refs[:3]
        cells, slots = refs[-2:]
        out_refs = refs[-2 - PLANES : -2]
    slots[...] = jnp.zeros_like(slots)
    cell = lax.broadcasted_iota(jnp.int32, (BLOCKS * CELL, TILE), 0)
    loaders = LOADERS // TILES
    count = TILE // loaders
    for t in range(TILES):
        rows = jnp.concatenate(
            [rows_ref[t * loaders + j, :count, :] for j in range(loaders)], axis=0
        )
        pick = jnp.where(cell == cell_ref[t : t + 1, :], 1.0, 0.0).astype(jnp.bfloat16)
        sorted_rows = jnp.dot(pick, rows, preferred_element_type=jnp.float32).astype(jnp.bfloat16)
        for b in range(BLOCKS):
            at = b * STRIP + t * CELL
            cells[at : at + CELL, :] = sorted_rows[b * CELL : (b + 1) * CELL, :]
        if tailed:
            sorted_labels = lax.dot_general(
                pick, label_ref[t], (((1,), (1,)), ((), ())), preferred_element_type=jnp.float32
            ).astype(jnp.bfloat16)
            for b in range(BLOCKS):
                at = b * STRIP + t * CELL
                label_cells[at : at + CELL, :] = sorted_labels[b * CELL : (b + 1) * CELL, :]
    step = lax.broadcasted_iota(jnp.int32, (SPAN, STRIP), 0)
    for b in range(BLOCKS):
        pick = jnp.where(step == strip_ref[b : b + 1, :], 1.0, 0.0).astype(jnp.bfloat16)
        strip = slice(b * STRIP, (b + 1) * STRIP)
        dense = jnp.dot(pick, cells[strip, :], preferred_element_type=jnp.float32).astype(
            jnp.bfloat16
        )
        first = pl.multiple_of(firsts[b], CELL)
        slots[pl.ds(first, CELL), :] += dense[:CELL, :]
        slots[pl.ds(first + CELL, SPAN - CELL), :] = dense[CELL:, :]
        if tailed:
            dense = jnp.dot(pick, label_cells[strip, :], preferred_element_type=jnp.float32)
            label_slots[pl.ds(first, CELL), :] += dense[:CELL, :]
            label_slots[pl.ds(first + CELL, SPAN - CELL), :] = dense[CELL:, :]
    for k in range(PLANES):
        out_refs[k][:ROOM, :] = slots[k * ROOM : (k + 1) * ROOM, :]
        if tailed:
            line = jnp.transpose(label_slots[k * ROOM : k * ROOM + ROOM_PAD, :])[:2, :]
            rows = [line[:, i * WIDE : (i + 1) * WIDE] for i in range(ROOM_PAD // WIDE)]
            flag = jnp.full((TAIL - 2 * len(rows), WIDE), over[0], jnp.int32).astype(jnp.float32)
            out_refs[k][ROOM:, :] = jnp.concatenate(rows + [flag], axis=0).astype(jnp.bfloat16)


def pack(firsts, cell, strip, rows, labels=None, over=None, after=()):
    tailed = labels is not None
    height = ROOM + TAIL if tailed else ROOM
    label_scratch = [
        pltpu.VMEM((BLOCKS * STRIP, DH), jnp.bfloat16),
        pltpu.VMEM((PLANES * ROOM + ROOM_PAD - ROOM + CELL, DH), jnp.float32),
    ]
    return pl.pallas_call(
        lambda *refs: pack_kernel(tailed, *refs),
        out_shape=[jax.ShapeDtypeStruct((height, WIDE), jnp.bfloat16)] * PLANES,
        in_specs=[in_smem()] * (2 if tailed else 1)
        + [pl.BlockSpec(memory_space=pltpu.VMEM)] * (4 if tailed else 3)
        + anywhere(len(after)),
        out_specs=[pl.BlockSpec(memory_space=pltpu.VMEM)] * PLANES,
        scratch_shapes=[
            pltpu.VMEM((BLOCKS * STRIP, WIDE), jnp.bfloat16),
            pltpu.VMEM((PLANES * ROOM + SPAN, WIDE), jnp.bfloat16),
        ]
        + (label_scratch if tailed else []),
        compiler_params=params(),
        cost_estimate=cost(2 * PLANE_ROWS * BLOCKS * CELL * WIDE, 16 << 20),
        name="pack",
    )(*((firsts, over, cell, strip, labels, rows) if tailed else (firsts, cell, strip, rows)), *after)


def gather_near(pieces, first, b, near, cols):
    for k in range(PLANES):
        from_row = pl.ds(pl.multiple_of(first[k * INNER + b], CELL), SPAN)
        near[k * SPAN : (k + 1) * SPAN, cols] = pieces[k][from_row, :]


def state_kernel(first, last_local, pos_ref, start_ref, *rest):
    key_pieces, value_pieces = rest[:PLANES], rest[PLANES : 2 * PLANES]
    choice_ref, mask_ref, use_ref, key_out, value_out, prior_out, end_out, near, state = rest[
        2 * PLANES :
    ]
    b = pl.program_id(0)

    @pl.when(b == 0)
    def _():
        state[...] = jnp.zeros_like(state)

    lane = lax.broadcasted_iota(jnp.int32, (PLANES, CHOICE), 1)
    line = jnp.full((1, CHOICE), -1, jnp.int32)
    for k in range(PLANES):
        shift = (k * SPAN - first[k * INNER + b] + CHOICE) % CHOICE
        rolled = pltpu.roll(pos_ref[...], shift, 1)
        inside = (lane >= k * SPAN) & (lane < (k + 1) * SPAN)
        line = jnp.where(inside, rolled, line)[k : k + 1, :] if k == 0 else jnp.where(
            inside[:1], rolled[k : k + 1, :], line
        )
    row = lax.broadcasted_iota(jnp.int32, (OWNED, CHOICE), 0)
    choice_ref[0] = jnp.where(row == line - b * OWNED, 1.0, 0.0).astype(jnp.bfloat16)
    gather_near(key_pieces, first, b, near, slice(0, WIDE))
    gather_near(value_pieces, first, b, near, slice(WIDE, 2 * WIDE))
    both = jnp.dot(choice_ref[0], near[...], preferred_element_type=jnp.float32).astype(jnp.bfloat16)
    keys, values = both[:, :WIDE], both[:, WIDE:]
    key_out[...] = keys
    value_out[...] = values
    index = lax.broadcasted_iota(jnp.int32, (OWNED, WIDE), 0)
    live = jnp.where(index >= last_local[b], keys, jnp.zeros_like(keys))
    keep = jnp.where(last_local[b] >= 0, 0.0, 1.0)
    for h in range(2):
        cols = slice(h * DH, (h + 1) * DH)
        fresh = lax.dot_general(
            live[:, cols],
            values[:, cols],
            (((0,), (0,)), ((), ())),
            preferred_element_type=jnp.float32,
        )
        before = state[h]
        prior_out[0, h] = before
        state[h] = fresh + keep * before
    end_out[...] = state[...]
    row = lax.broadcasted_iota(jnp.int32, (OWNED, OWNED), 0)
    column = lax.broadcasted_iota(jnp.int32, (OWNED, OWNED), 1)
    allowed = (column <= row) & (column >= start_ref[...])
    mask_ref[0] = jnp.where(allowed, 1.0, 0.0).astype(jnp.bfloat16)
    before = jnp.broadcast_to(start_ref[...], (OWNED, DH)) < 0
    use_ref[...] = jnp.where(before, 1.0, 0.0).astype(jnp.bfloat16)


def states(first, last_local, pos, starts, key_pieces, value_pieces):
    full = jax.ShapeDtypeStruct((PLANE_ROWS, WIDE), jnp.bfloat16)
    return pl.pallas_call(
        state_kernel,
        grid=(INNER,),
        out_shape=[
            jax.ShapeDtypeStruct((INNER, OWNED, CHOICE), jnp.bfloat16),
            jax.ShapeDtypeStruct((INNER, OWNED, OWNED), jnp.bfloat16),
            jax.ShapeDtypeStruct((PLANE_ROWS, DH), jnp.bfloat16),
            full,
            full,
            jax.ShapeDtypeStruct((INNER, 2, DH, DH), jnp.float32),
            jax.ShapeDtypeStruct((2, DH, DH), jnp.float32),
        ],
        in_specs=[
            in_smem(),
            in_smem(),
            whole(PLANES, CHOICE),
            pl.BlockSpec((OWNED, 1), lambda i: (i, 0)),
        ]
        + [whole(ROOM, WIDE)] * PLANES
        + [whole(ROOM + TAIL, WIDE)] * PLANES,
        out_specs=[
            pl.BlockSpec((1, OWNED, CHOICE), lambda i: (i, 0, 0)),
            pl.BlockSpec((1, OWNED, OWNED), lambda i: (i, 0, 0)),
            pl.BlockSpec((OWNED, DH), lambda i: (i, 0)),
            pl.BlockSpec((OWNED, WIDE), lambda i: (i, 0)),
            pl.BlockSpec((OWNED, WIDE), lambda i: (i, 0)),
            pl.BlockSpec((1, 2, DH, DH), lambda i: (i, 0, 0, 0)),
            whole(2, DH, DH),
        ],
        scratch_shapes=[
            pltpu.VMEM((CHOICE, 2 * WIDE), jnp.bfloat16),
            pltpu.VMEM((2, DH, DH), jnp.float32),
        ],
        compiler_params=params(),
        cost_estimate=cost(4 * PLANE_ROWS * CHOICE * WIDE, 30 << 20),
        name="states",
    )(first, last_local, pos, starts, *key_pieces, *value_pieces)


def attend_kernel(first, carries, choice_ref, mask_ref, use_ref, gain_ref, key_ref, value_ref,
                  prior_ref, entry_ref, *rest):
    query_pieces = rest[:PLANES]
    out_ref, near, held = rest[PLANES:]
    half = OWNED // 2
    step = pl.program_id(0)
    b = jnp.maximum(step - 1, 0)
    queries = held[lax.rem(step + 1, 2)]
    gather_near(query_pieces, first, jnp.minimum(step, INNER - 1), near, slice(0, WIDE))
    held[lax.rem(step, 2)] = jnp.dot(
        choice_ref[0], near[...], preferred_element_type=jnp.float32
    ).astype(jnp.bfloat16)
    carried_in = carries[b].astype(jnp.float32)
    for h in range(2):
        cols = slice(h * DH, (h + 1) * DH)
        prior = (prior_ref[0, h] + carried_in * entry_ref[h]).astype(jnp.bfloat16)
        for part in range(2):
            width = (part + 1) * half
            rows = slice(part * half, (part + 1) * half)
            query = queries[rows, cols]
            scores = lax.dot_general(
                query, key_ref[:width, cols], (((1,), (1,)), ((), ())),
                preferred_element_type=jnp.float32,
            )
            weights = scores.astype(jnp.bfloat16) * mask_ref[0, rows, :width]
            combined = jnp.dot(
                weights, value_ref[:width, cols], preferred_element_type=jnp.float32
            ) + jnp.dot(query * use_ref[rows, :], prior, preferred_element_type=jnp.float32)
            square = jnp.mean(combined * combined, axis=-1, keepdims=True)
            result = combined * lax.rsqrt(square + 1e-06) * gain_ref[:, cols]
            out_ref[0, rows, cols] = result.astype(jnp.bfloat16)


def attend(first, carries, choice, mask, use, gain, keys, values, prior, entry, query_pieces):
    return pl.pallas_call(
        attend_kernel,
        grid=(INNER + 1,),
        out_shape=jax.ShapeDtypeStruct((INNER, OWNED, WIDE), jnp.bfloat16),
        in_specs=[
            in_smem(),
            in_smem(),
            pl.BlockSpec((1, OWNED, CHOICE), lambda i: (jnp.minimum(i, INNER - 1), 0, 0)),
            pl.BlockSpec((1, OWNED, OWNED), lambda i: (jnp.maximum(i - 1, 0), 0, 0)),
            pl.BlockSpec((OWNED, DH), lambda i: (jnp.maximum(i - 1, 0), 0)),
            whole(1, WIDE),
            pl.BlockSpec((OWNED, WIDE), lambda i: (jnp.maximum(i - 1, 0), 0)),
            pl.BlockSpec((OWNED, WIDE), lambda i: (jnp.maximum(i - 1, 0), 0)),
            pl.BlockSpec((1, 2, DH, DH), lambda i: (jnp.maximum(i - 1, 0), 0, 0, 0)),
            whole(2, DH, DH),
        ]
        + [whole(ROOM, WIDE)] * PLANES,
        out_specs=pl.BlockSpec((1, OWNED, WIDE), lambda i: (jnp.maximum(i - 1, 0), 0, 0)),
        scratch_shapes=[
            pltpu.VMEM((CHOICE, WIDE), jnp.bfloat16),
            pltpu.VMEM((2, OWNED, WIDE), jnp.bfloat16),
        ],
        compiler_params=params(),
        cost_estimate=cost(4 * PLANE_ROWS * CHOICE * WIDE, 30 << 20),
        name="attend",
    )(first, carries, choice, mask, use, gain, keys, values, prior, entry, *query_pieces)


def join_kernel(in_ref, out_ref):
    for i in range(INNER):
        out_ref[:, i * WIDE : (i + 1) * WIDE] = in_ref[i]


def join(parts):
    return pl.pallas_call(
        join_kernel,
        out_shape=jax.ShapeDtypeStruct((OWNED, INNER * WIDE), jnp.bfloat16),
        in_specs=[pl.BlockSpec(memory_space=pltpu.VMEM)],
        out_specs=pl.BlockSpec(memory_space=pltpu.VMEM),
        compiler_params=params(),
        cost_estimate=cost(0, 4 << 20),
        name="join",
    )(parts)


def spread(parts):
    return lax.all_to_all(parts, LOCAL, split_axis=0, concat_axis=0, tiled=True)


def along(pieces, before=()):
    moved = {0: pieces[0]}
    for k in ORDER:
        first = (moved[AHEAD[k]],) if k in AHEAD else before
        piece, _ = lax.optimization_barrier((pieces[k], first))
        pairs = [(i, (i + k) % PLANES) for i in range(PLANES)]
        moved[k] = lax.ppermute(piece, "z", pairs)
    return [moved[k] for k in range(PLANES)]


def slotting(places, plane):
    owner = places // OWNED
    shift = (owner // INNER - plane) % PLANES
    block = (shift * INNER + owner % INNER).reshape(TILES, TILE)
    same = block[:, :, None] == block[:, None, :]
    at = jnp.arange(TILE)
    within = jnp.sum((same & (at[None, :] < at[:, None])[None]).astype(jnp.int32), axis=2)
    onehot = (block[:, :, None] == jnp.arange(BLOCKS)[None, None, :]).astype(jnp.int32)
    counts = jnp.sum(onehot, axis=1)
    tile_at = jnp.arange(TILES)
    earlier = jnp.sum(
        jnp.where((tile_at[None, :] < tile_at[:, None])[:, :, None], counts[None], 0), axis=1
    )
    totals = jnp.sum(counts, axis=0)
    block_at = jnp.arange(BLOCKS)
    sooner = (block_at[None, :] < block_at[:, None]) & (
        block_at[None, :] // INNER == block_at[:, None] // INNER
    )
    base = jnp.sum(jnp.where(sooner, totals[None, :], 0), axis=1)
    start = earlier + (base + block_at // INNER * ROOM)[None, :]
    firsts = jnp.minimum(start[0] // CELL * CELL, PLANES * ROOM).astype(jnp.int32)
    inside = jnp.arange(CELL)
    strip = jnp.where(
        inside[None, None, :] < counts.T[:, :, None],
        (start - firsts[None, :]).T[:, :, None] + inside[None, None, :],
        -1,
    ).reshape(BLOCKS, STRIP)
    cell = block * CELL + within
    over = jnp.any(jnp.sum(totals.reshape(PLANES, INNER), axis=1) > ROOM).astype(jnp.int32)
    return cell.astype(jnp.int32), strip.astype(jnp.int32), firsts, over.reshape(1)


def label(places):
    value = (places % PLANE_ROWS + 1).reshape(TILES, 1, TILE)
    digit = jnp.arange(DH)[None, :, None]
    return jnp.where(
        digit == 0, value // 64, jnp.where(digit == 1, value % 64, 0)
    ).astype(jnp.bfloat16)


def read_labels(tails):
    line = tails[:, : 2 * (ROOM_PAD // WIDE), :].reshape(PLANES, ROOM_PAD // WIDE, 2, WIDE)
    line = jnp.transpose(line, (0, 2, 1, 3)).reshape(PLANES, 2, ROOM_PAD).astype(jnp.int32)
    pos = (line[:, 0, :] * 64 + line[:, 1, :] - 1)[:, :ROOM]
    over = jnp.max(tails[:, TAIL - 1, 0]).astype(jnp.int32)
    begin = jnp.arange(INNER) * OWNED
    ahead = jnp.sum(
        ((pos[:, None, :] >= 0) & (pos[:, None, :] < begin[None, :, None])).astype(jnp.int32), axis=2
    )
    first = jnp.minimum(ahead // CELL * CELL, ROOM - SPAN).astype(jnp.int32).reshape(-1)
    pos = jnp.pad(pos, ((0, 0), (0, CHOICE - ROOM)), constant_values=-1)
    return pos, first, over


def shards(query_rows, key_rows, value_rows, destination, doc_lengths, norm_gain):
    plane = lax.axis_index("z")
    inner = lax.axis_index("a")
    count = destination.shape[0]
    digits = jnp.concatenate([destination // WIDE, destination % WIDE]).astype(jnp.bfloat16)
    spare = jnp.pad(digits[None], ((0, CELL - 1), (0, 0)))
    key_rows_there = spread(split(key_rows, (), spare))
    digits = key_rows_there[:, count, :].astype(jnp.int32)
    places = (digits[:, :count] * WIDE + digits[:, count:]).reshape(-1)
    cell, strip, firsts, over = slotting(places, plane)
    value_rows_there = spread(split(value_rows, (cell, strip)))
    key_pieces = along(pack(firsts, cell, strip, key_rows_there))
    value_packed = pack(firsts, cell, strip, value_rows_there, label(places), over)
    query_rows_there = spread(split(query_rows, (value_packed[0], *key_pieces[1:])))
    value_pieces = along(value_packed, tuple(key_pieces[1:]))
    query_packed = pack(firsts, cell, strip, query_rows_there, after=value_pieces[1:])
    query_pieces = along(query_packed)
    doc_lengths_then, _ = lax.optimization_barrier((doc_lengths, key_pieces[1]))
    value_pieces[0], _ = lax.optimization_barrier(
        (value_pieces[0], (query_pieces[1], query_pieces[7]))
    )
    pos, first, any_over = read_labels(jnp.stack([piece[ROOM:] for piece in value_pieces]))

    doc_ends = jnp.cumsum(doc_lengths_then)
    doc_begins = doc_ends - doc_lengths_then
    positions = plane * PLANE_ROWS + jnp.arange(PLANE_ROWS, dtype=jnp.int32)
    doc_start = jnp.max(
        jnp.where(doc_begins[None, :] <= positions[:, None], doc_begins[None, :], 0), axis=1
    )
    local_start = (doc_start - positions // OWNED * OWNED).astype(jnp.int32)
    last_local = local_start.reshape(INNER, OWNED)[:, OWNED - 1]
    block_at = jnp.arange(INNER)
    carries = jnp.all(
        (block_at[None, :] >= block_at[:, None]) | (last_local[None, :] < 0), axis=1
    ).astype(jnp.int32)

    choice, mask, use, keys, values, prior, end = states(
        first, last_local, pos, local_start[:, None], key_pieces, value_pieces
    )
    entry = lax.ppermute(end, "z", [(i, i + 1) for i in range(PLANES - 1)])
    gain = lax.dynamic_slice_in_dim(norm_gain.astype(jnp.float32), inner * WIDE, WIDE).reshape(1, WIDE)
    attended = attend(
        first, carries, choice, mask, use, gain, keys, values, prior, entry, query_pieces
    )
    back = lax.all_to_all(attended, "a", split_axis=0, concat_axis=0, tiled=True)
    return lax.cond(
        any_over > 0,
        lambda: direct(query_rows, key_rows, value_rows, destination, doc_lengths, norm_gain),
        lambda: join(back),
    )


def solution(mesh):
    fine = Mesh(mesh.devices.reshape(PLANES, INNER, mesh.shape["head"]), ("z", "a", "head"))
    every = ("z", "a", "head")
    in_specs = (P(every, None), P(every, None), P(every, None), P(every), P(), P("head"))
    return jax.shard_map(
        shards, mesh=fine, in_specs=in_specs, out_specs=P(SEQ, "head"), check_vma=False
    )
```

```python
import jax
import jax.numpy as jnp
from jax import lax
from jax.experimental import pallas as pl
from jax.experimental.pallas import tpu as pltpu
from jax.sharding import Mesh
from jax.sharding import PartitionSpec as P

DH = 128
OWNED = 512
PLANES = 8
INNER = 8
PLANE_ROWS = INNER * OWNED
WIDE = 2 * DH
LOADERS = 32
ROOM = 592
ROOM_PAD = 768
TAIL = 16
TILE = 512
TILES = PLANE_ROWS // TILE
BLOCKS = PLANES * INNER
CELL = 16
STRIP = TILES * CELL
SPAN = 144
CHOICE = PLANES * SPAN
ORDER = (3, 5, 1, 7, 4, 2, 6)
AHEAD = {2: 1, 6: 7}
SEQ = ("z", "a")
LOCAL = ("head", "a")
VMEM_LIMIT = 56 * 1024 * 1024


def entering(part, axis, combine, identity):
    place = lax.axis_index(axis)
    gathered = jax.tree.map(lambda a: lax.all_gather(a, axis), part)
    state = jax.tree.map(lambda a, e: jnp.zeros_like(a) + jnp.asarray(e, a.dtype), part, identity)

    def one(step, state):
        return combine(
            state, jax.tree.map(lambda a: lax.dynamic_index_in_dim(a, step, 0, False), gathered)
        )

    return lax.fori_loop(0, place, one, state)


def build_slots(tensors, targets, owners, slots, owned):
    owner_index = targets // owned
    onehot = (owner_index[:, None] == jnp.arange(owners, dtype=jnp.int32)[None, :]).astype(
        jnp.int32
    )
    rank_within = jnp.sum((jnp.cumsum(onehot, axis=0) - 1) * onehot, axis=1)
    slot_index = owner_index * slots + rank_within
    buffers = tuple(
        (
            jnp.zeros((owners * slots, tensor.shape[1]), tensor.dtype)
            .at[slot_index]
            .set(tensor)
            .reshape(owners, slots, tensor.shape[1])
            for tensor in tensors
        )
    )
    where_to = (
        jnp.full((owners * slots,), -1, jnp.int32)
        .at[slot_index]
        .set(targets)
        .reshape(owners, slots)
    )
    return (buffers, where_to)


def settle(arrived, where_to, owned, begin):
    local_place = where_to.reshape(-1) - begin
    local_place = jnp.where(where_to.reshape(-1) < 0, owned, local_place).astype(jnp.int32)
    flat = arrived.reshape(-1, arrived.shape[-1])
    return jnp.zeros((owned + 1, flat.shape[1]), flat.dtype).at[local_place].set(flat)[:owned]


def direct(query_rows, key_rows, value_rows, destination, doc_lengths, norm_gain):
    n_seq = lax.axis_size(SEQ)
    n_head = lax.axis_size("head")
    loader_rows = query_rows.shape[0]
    owned = loader_rows * n_head
    narrow = query_rows.shape[1] // n_head
    local_heads = narrow // DH
    capacity = 2 * loader_rows // n_seq
    begin = lax.axis_index(SEQ) * owned
    split_q, split_k, split_v = (
        lax.all_to_all(query_rows, "head", split_axis=1, concat_axis=0, tiled=True),
        lax.all_to_all(key_rows, "head", split_axis=1, concat_axis=0, tiled=True),
        lax.all_to_all(value_rows, "head", split_axis=1, concat_axis=0, tiled=True),
    )
    group_dest = lax.all_gather(destination, "head", axis=0, tiled=True)
    buffers, where_to = build_slots(
        (split_q, split_k, split_v), group_dest, n_seq, n_head * capacity, owned
    )
    got_q, got_k, got_v, got_where = (
        lax.all_to_all(buffers[0], SEQ, split_axis=0, concat_axis=0, tiled=True),
        lax.all_to_all(buffers[1], SEQ, split_axis=0, concat_axis=0, tiled=True),
        lax.all_to_all(buffers[2], SEQ, split_axis=0, concat_axis=0, tiled=True),
        lax.all_to_all(where_to, SEQ, split_axis=0, concat_axis=0, tiled=True),
    )
    seq_query = settle(got_q, got_where, owned, begin).reshape(owned, local_heads, DH)
    seq_key = settle(got_k, got_where, owned, begin).reshape(owned, local_heads, DH)
    seq_value = settle(got_v, got_where, owned, begin).reshape(owned, local_heads, DH)
    doc_ends = jnp.cumsum(doc_lengths)
    doc_begins = doc_ends - doc_lengths
    local_index = jnp.arange(owned, dtype=jnp.int32)
    positions = begin + local_index
    doc_start = jnp.max(
        jnp.where(doc_begins[None, :] <= positions[:, None], doc_begins[None, :], 0), axis=1
    )
    allowed = (local_index[None, :] <= local_index[:, None]) & (
        positions[None, :] >= doc_start[:, None]
    )
    scores = jnp.einsum("qhd,khd->hqk", seq_query, seq_key, preferred_element_type=jnp.float32)
    weights = jnp.where(allowed[None], scores, 0.0).astype(jnp.bfloat16)
    intra = jnp.einsum("hqk,khd->qhd", weights, seq_value, preferred_element_type=jnp.float32)
    last_start = doc_start[owned - 1]
    live_keys = (positions >= last_start).astype(jnp.bfloat16)
    local_state = jnp.einsum(
        "khd,khe->hde",
        seq_key * live_keys[:, None, None],
        seq_value,
        preferred_element_type=jnp.float32,
    )
    restart = jnp.reshape((last_start >= begin).astype(jnp.float32), (1,))

    def combine_states(earlier, later):
        return (later[0] + (1.0 - later[1][0]) * earlier[0], jnp.maximum(earlier[1], later[1]))

    identity = (jnp.zeros_like(local_state), jnp.zeros((1,), jnp.float32))
    prior, _ = entering((local_state, restart), SEQ, combine_states, identity)
    prior_low = prior.astype(jnp.bfloat16)
    carried = jnp.einsum("qhd,hde->qhe", seq_query, prior_low, preferred_element_type=jnp.float32)
    use_prior = (doc_start < begin).astype(jnp.float32)
    combined = intra + use_prior[:, None, None] * carried
    mean_square = jnp.mean(combined * combined, axis=-1, keepdims=True)
    gain_wide = norm_gain.astype(jnp.float32).reshape(local_heads, DH)
    result = combined * lax.rsqrt(mean_square + 1e-06) * gain_wide
    return result.astype(jnp.bfloat16).reshape(owned, narrow)


def whole(*shape):
    return pl.BlockSpec(shape, lambda *_: (0,) * len(shape))


def in_smem():
    return pl.BlockSpec(memory_space=pltpu.SMEM)


def anywhere(count):
    return [pl.BlockSpec(memory_space=pl.ANY)] * count


def params():
    return pltpu.CompilerParams(vmem_limit_bytes=VMEM_LIMIT)


def cost(flops, size):
    return pl.CostEstimate(flops=flops, bytes_accessed=size, transcendentals=0)


def split_kernel(labelled, in_ref, *rest):
    out_ref = rest[-1]
    count = in_ref.shape[0]
    for i in range(LOADERS):
        out_ref[i, :count, :] = in_ref[:, i * WIDE : (i + 1) * WIDE]
        if labelled:
            out_ref[i, count:, :] = rest[0][...]


def split(rows, after=(), spare=None):
    labelled = spare is not None
    count = rows.shape[0] + (spare.shape[0] if labelled else 0)
    return pl.pallas_call(
        lambda *refs: split_kernel(labelled, *refs),
        out_shape=jax.ShapeDtypeStruct((LOADERS, count, WIDE), rows.dtype),
        in_specs=[pl.BlockSpec(memory_space=pltpu.VMEM)] * (2 if labelled else 1)
        + anywhere(len(after)),
        out_specs=pl.BlockSpec(memory_space=pltpu.VMEM),
        compiler_params=params(),
        cost_estimate=cost(0, 4 << 20),
        name="split",
    )(rows, *((spare,) if labelled else ()), *after)


def pack_kernel(tailed, firsts, *refs):
    if tailed:
        over, cell_ref, strip_ref, label_ref, rows_ref = refs[:5]
        cells, slots, label_cells, label_slots = refs[-4:]
        out_refs = refs[-4 - PLANES : -4]
        label_slots[...] = jnp.zeros_like(label_slots)
    else:
        cell_ref, strip_ref, rows_ref = refs[:3]
        cells, slots = refs[-2:]
        out_refs = refs[-2 - PLANES : -2]
    slots[...] = jnp.zeros_like(slots)
    cell = lax.broadcasted_iota(jnp.int32, (BLOCKS * CELL, TILE), 0)
    loaders = LOADERS // TILES
    count = TILE // loaders
    for t in range(TILES):
        rows = jnp.concatenate(
            [rows_ref[t * loaders + j, :count, :] for j in range(loaders)], axis=0
        )
        pick = jnp.where(cell == cell_ref[t : t + 1, :], 1.0, 0.0).astype(jnp.bfloat16)
        sorted_rows = jnp.dot(pick, rows, preferred_element_type=jnp.float32).astype(jnp.bfloat16)
        for b in range(BLOCKS):
            at = b * STRIP + t * CELL
            cells[at : at + CELL, :] = sorted_rows[b * CELL : (b + 1) * CELL, :]
        if tailed:
            sorted_labels = lax.dot_general(
                pick, label_ref[t], (((1,), (1,)), ((), ())), preferred_element_type=jnp.float32
            ).astype(jnp.bfloat16)
            for b in range(BLOCKS):
                at = b * STRIP + t * CELL
                label_cells[at : at + CELL, :] = sorted_labels[b * CELL : (b + 1) * CELL, :]
    step = lax.broadcasted_iota(jnp.int32, (SPAN, STRIP), 0)
    for b in range(BLOCKS):
        pick = jnp.where(step == strip_ref[b : b + 1, :], 1.0, 0.0).astype(jnp.bfloat16)
        strip = slice(b * STRIP, (b + 1) * STRIP)
        dense = jnp.dot(pick, cells[strip, :], preferred_element_type=jnp.float32).astype(
            jnp.bfloat16
        )
        first = pl.multiple_of(firsts[b], CELL)
        slots[pl.ds(first, CELL), :] += dense[:CELL, :]
        slots[pl.ds(first + CELL, SPAN - CELL), :] = dense[CELL:, :]
        if tailed:
            dense = jnp.dot(pick, label_cells[strip, :], preferred_element_type=jnp.float32)
            label_slots[pl.ds(first, CELL), :] += dense[:CELL, :]
            label_slots[pl.ds(first + CELL, SPAN - CELL), :] = dense[CELL:, :]
    for k in range(PLANES):
        out_refs[k][:ROOM, :] = slots[k * ROOM : (k + 1) * ROOM, :]
        if tailed:
            line = jnp.transpose(label_slots[k * ROOM : k * ROOM + ROOM_PAD, :])[:2, :]
            rows = [line[:, i * WIDE : (i + 1) * WIDE] for i in range(ROOM_PAD // WIDE)]
            flag = jnp.full((TAIL - 2 * len(rows), WIDE), over[0], jnp.int32).astype(jnp.float32)
            out_refs[k][ROOM:, :] = jnp.concatenate(rows + [flag], axis=0).astype(jnp.bfloat16)


def pack(firsts, cell, strip, rows, labels=None, over=None, after=()):
    tailed = labels is not None
    height = ROOM + TAIL if tailed else ROOM
    label_scratch = [
        pltpu.VMEM((BLOCKS * STRIP, DH), jnp.bfloat16),
        pltpu.VMEM((PLANES * ROOM + ROOM_PAD - ROOM + CELL, DH), jnp.float32),
    ]
    return pl.pallas_call(
        lambda *refs: pack_kernel(tailed, *refs),
        out_shape=[jax.ShapeDtypeStruct((height, WIDE), jnp.bfloat16)] * PLANES,
        in_specs=[in_smem()] * (2 if tailed else 1)
        + [pl.BlockSpec(memory_space=pltpu.VMEM)] * (4 if tailed else 3)
        + anywhere(len(after)),
        out_specs=[pl.BlockSpec(memory_space=pltpu.VMEM)] * PLANES,
        scratch_shapes=[
            pltpu.VMEM((BLOCKS * STRIP, WIDE), jnp.bfloat16),
            pltpu.VMEM((PLANES * ROOM + SPAN, WIDE), jnp.bfloat16),
        ]
        + (label_scratch if tailed else []),
        compiler_params=params(),
        cost_estimate=cost(2 * PLANE_ROWS * BLOCKS * CELL * WIDE, 16 << 20),
        name="pack",
    )(*((firsts, over, cell, strip, labels, rows) if tailed else (firsts, cell, strip, rows)), *after)


def gather_near(pieces, first, b, near, cols):
    for k in range(PLANES):
        from_row = pl.ds(pl.multiple_of(first[k * INNER + b], CELL), SPAN)
        near[k * SPAN : (k + 1) * SPAN, cols] = pieces[k][from_row, :]


def state_kernel(first, last_local, pos_ref, start_ref, *rest):
    key_pieces, value_pieces = rest[:PLANES], rest[PLANES : 2 * PLANES]
    choice_ref, mask_ref, use_ref, key_out, value_out, prior_out, end_out, near, state = rest[
        2 * PLANES :
    ]
    b = pl.program_id(0)

    @pl.when(b == 0)
    def _():
        state[...] = jnp.zeros_like(state)

    lane = lax.broadcasted_iota(jnp.int32, (PLANES, CHOICE), 1)
    line = jnp.full((1, CHOICE), -1, jnp.int32)
    for k in range(PLANES):
        shift = (k * SPAN - first[k * INNER + b] + CHOICE) % CHOICE
        rolled = pltpu.roll(pos_ref[...], shift, 1)
        inside = (lane >= k * SPAN) & (lane < (k + 1) * SPAN)
        line = jnp.where(inside, rolled, line)[k : k + 1, :] if k == 0 else jnp.where(
            inside[:1], rolled[k : k + 1, :], line
        )
    row = lax.broadcasted_iota(jnp.int32, (OWNED, CHOICE), 0)
    choice_ref[0] = jnp.where(row == line - b * OWNED, 1.0, 0.0).astype(jnp.bfloat16)
    gather_near(key_pieces, first, b, near, slice(0, WIDE))
    gather_near(value_pieces, first, b, near, slice(WIDE, 2 * WIDE))
    both = jnp.dot(choice_ref[0], near[...], preferred_element_type=jnp.float32).astype(jnp.bfloat16)
    keys, values = both[:, :WIDE], both[:, WIDE:]
    key_out[...] = keys
    value_out[...] = values
    index = lax.broadcasted_iota(jnp.int32, (OWNED, WIDE), 0)
    live = jnp.where(index >= last_local[b], keys, jnp.zeros_like(keys))
    keep = jnp.where(last_local[b] >= 0, 0.0, 1.0)
    for h in range(2):
        cols = slice(h * DH, (h + 1) * DH)
        fresh = lax.dot_general(
            live[:, cols],
            values[:, cols],
            (((0,), (0,)), ((), ())),
            preferred_element_type=jnp.float32,
        )
        before = state[h]
        prior_out[0, h] = before
        state[h] = fresh + keep * before
    end_out[...] = state[...]
    row = lax.broadcasted_iota(jnp.int32, (OWNED, OWNED), 0)
    column = lax.broadcasted_iota(jnp.int32, (OWNED, OWNED), 1)
    allowed = (column <= row) & (column >= start_ref[...])
    mask_ref[0] = jnp.where(allowed, 1.0, 0.0).astype(jnp.bfloat16)
    before = jnp.broadcast_to(start_ref[...], (OWNED, DH)) < 0
    use_ref[...] = jnp.where(before, 1.0, 0.0).astype(jnp.bfloat16)


def states(first, last_local, pos, starts, key_pieces, value_pieces):
    full = jax.ShapeDtypeStruct((PLANE_ROWS, WIDE), jnp.bfloat16)
    return pl.pallas_call(
        state_kernel,
        grid=(INNER,),
        out_shape=[
            jax.ShapeDtypeStruct((INNER, OWNED, CHOICE), jnp.bfloat16),
            jax.ShapeDtypeStruct((INNER, OWNED, OWNED), jnp.bfloat16),
            jax.ShapeDtypeStruct((PLANE_ROWS, DH), jnp.bfloat16),
            full,
            full,
            jax.ShapeDtypeStruct((INNER, 2, DH, DH), jnp.float32),
            jax.ShapeDtypeStruct((2, DH, DH), jnp.float32),
        ],
        in_specs=[
            in_smem(),
            in_smem(),
            whole(PLANES, CHOICE),
            pl.BlockSpec((OWNED, 1), lambda i: (i, 0)),
        ]
        + [whole(ROOM, WIDE)] * PLANES
        + [whole(ROOM + TAIL, WIDE)] * PLANES,
        out_specs=[
            pl.BlockSpec((1, OWNED, CHOICE), lambda i: (i, 0, 0)),
            pl.BlockSpec((1, OWNED, OWNED), lambda i: (i, 0, 0)),
            pl.BlockSpec((OWNED, DH), lambda i: (i, 0)),
            pl.BlockSpec((OWNED, WIDE), lambda i: (i, 0)),
            pl.BlockSpec((OWNED, WIDE), lambda i: (i, 0)),
            pl.BlockSpec((1, 2, DH, DH), lambda i: (i, 0, 0, 0)),
            whole(2, DH, DH),
        ],
        scratch_shapes=[
            pltpu.VMEM((CHOICE, 2 * WIDE), jnp.bfloat16),
            pltpu.VMEM((2, DH, DH), jnp.float32),
        ],
        compiler_params=params(),
        cost_estimate=cost(4 * PLANE_ROWS * CHOICE * WIDE, 30 << 20),
        name="states",
    )(first, last_local, pos, starts, *key_pieces, *value_pieces)


def attend_kernel(first, carries, choice_ref, mask_ref, use_ref, gain_ref, key_ref, value_ref,
                  prior_ref, entry_ref, *rest):
    query_pieces = rest[:PLANES]
    out_ref, near, held = rest[PLANES:]
    half = OWNED // 2
    step = pl.program_id(0)
    b = jnp.maximum(step - 1, 0)
    queries = held[lax.rem(step + 1, 2)]
    gather_near(query_pieces, first, jnp.minimum(step, INNER - 1), near, slice(0, WIDE))
    held[lax.rem(step, 2)] = jnp.dot(
        choice_ref[0], near[...], preferred_element_type=jnp.float32
    ).astype(jnp.bfloat16)
    carried_in = carries[b].astype(jnp.float32)
    for h in range(2):
        cols = slice(h * DH, (h + 1) * DH)
        prior = (prior_ref[0, h] + carried_in * entry_ref[h]).astype(jnp.bfloat16)
        for part in range(2):
            width = (part + 1) * half
            rows = slice(part * half, (part + 1) * half)
            query = queries[rows, cols]
            scores = lax.dot_general(
                query, key_ref[:width, cols], (((1,), (1,)), ((), ())),
                preferred_element_type=jnp.float32,
            )
            weights = scores.astype(jnp.bfloat16) * mask_ref[0, rows, :width]
            combined = jnp.dot(
                weights, value_ref[:width, cols], preferred_element_type=jnp.float32
            ) + jnp.dot(query * use_ref[rows, :], prior, preferred_element_type=jnp.float32)
            square = jnp.mean(combined * combined, axis=-1, keepdims=True)
            result = combined * lax.rsqrt(square + 1e-06) * gain_ref[:, cols]
            out_ref[0, rows, cols] = result.astype(jnp.bfloat16)


def attend(first, carries, choice, mask, use, gain, keys, values, prior, entry, query_pieces):
    return pl.pallas_call(
        attend_kernel,
        grid=(INNER + 1,),
        out_shape=jax.ShapeDtypeStruct((INNER, OWNED, WIDE), jnp.bfloat16),
        in_specs=[
            in_smem(),
            in_smem(),
            pl.BlockSpec((1, OWNED, CHOICE), lambda i: (jnp.minimum(i, INNER - 1), 0, 0)),
            pl.BlockSpec((1, OWNED, OWNED), lambda i: (jnp.maximum(i - 1, 0), 0, 0)),
            pl.BlockSpec((OWNED, DH), lambda i: (jnp.maximum(i - 1, 0), 0)),
            whole(1, WIDE),
            pl.BlockSpec((OWNED, WIDE), lambda i: (jnp.maximum(i - 1, 0), 0)),
            pl.BlockSpec((OWNED, WIDE), lambda i: (jnp.maximum(i - 1, 0), 0)),
            pl.BlockSpec((1, 2, DH, DH), lambda i: (jnp.maximum(i - 1, 0), 0, 0, 0)),
            whole(2, DH, DH),
        ]
        + [whole(ROOM, WIDE)] * PLANES,
        out_specs=pl.BlockSpec((1, OWNED, WIDE), lambda i: (jnp.maximum(i - 1, 0), 0, 0)),
        scratch_shapes=[
            pltpu.VMEM((CHOICE, WIDE), jnp.bfloat16),
            pltpu.VMEM((2, OWNED, WIDE), jnp.bfloat16),
        ],
        compiler_params=params(),
        cost_estimate=cost(4 * PLANE_ROWS * CHOICE * WIDE, 30 << 20),
        name="attend",
    )(first, carries, choice, mask, use, gain, keys, values, prior, entry, *query_pieces)


def join_kernel(in_ref, out_ref):
    for i in range(INNER):
        out_ref[:, i * WIDE : (i + 1) * WIDE] = in_ref[i]


def join(parts):
    return pl.pallas_call(
        join_kernel,
        out_shape=jax.ShapeDtypeStruct((OWNED, INNER * WIDE), jnp.bfloat16),
        in_specs=[pl.BlockSpec(memory_space=pltpu.VMEM)],
        out_specs=pl.BlockSpec(memory_space=pltpu.VMEM),
        compiler_params=params(),
        cost_estimate=cost(0, 4 << 20),
        name="join",
    )(parts)


def spread(parts):
    return lax.all_to_all(parts, LOCAL, split_axis=0, concat_axis=0, tiled=True)


def along(pieces, before=()):
    moved = {0: pieces[0]}
    for k in ORDER:
        first = (moved[AHEAD[k]],) if k in AHEAD else before
        piece, _ = lax.optimization_barrier((pieces[k], first))
        pairs = [(i, (i + k) % PLANES) for i in range(PLANES)]
        moved[k] = lax.ppermute(piece, "z", pairs)
    return [moved[k] for k in range(PLANES)]


def slotting(places, plane):
    owner = places // OWNED
    shift = (owner // INNER - plane) % PLANES
    block = (shift * INNER + owner % INNER).reshape(TILES, TILE)
    same = block[:, :, None] == block[:, None, :]
    at = jnp.arange(TILE)
    within = jnp.sum((same & (at[None, :] < at[:, None])[None]).astype(jnp.int32), axis=2)
    onehot = (block[:, :, None] == jnp.arange(BLOCKS)[None, None, :]).astype(jnp.int32)
    counts = jnp.sum(onehot, axis=1)
    tile_at = jnp.arange(TILES)
    earlier = jnp.sum(
        jnp.where((tile_at[None, :] < tile_at[:, None])[:, :, None], counts[None], 0), axis=1
    )
    totals = jnp.sum(counts, axis=0)
    block_at = jnp.arange(BLOCKS)
    sooner = (block_at[None, :] < block_at[:, None]) & (
        block_at[None, :] // INNER == block_at[:, None] // INNER
    )
    base = jnp.sum(jnp.where(sooner, totals[None, :], 0), axis=1)
    start = earlier + (base + block_at // INNER * ROOM)[None, :]
    firsts = jnp.minimum(start[0] // CELL * CELL, PLANES * ROOM).astype(jnp.int32)
    inside = jnp.arange(CELL)
    strip = jnp.where(
        inside[None, None, :] < counts.T[:, :, None],
        (start - firsts[None, :]).T[:, :, None] + inside[None, None, :],
        -1,
    ).reshape(BLOCKS, STRIP)
    cell = block * CELL + within
    over = jnp.any(jnp.sum(totals.reshape(PLANES, INNER), axis=1) > ROOM).astype(jnp.int32)
    return cell.astype(jnp.int32), strip.astype(jnp.int32), firsts, over.reshape(1)


def label(places):
    value = (places % PLANE_ROWS + 1).reshape(TILES, 1, TILE)
    digit = jnp.arange(DH)[None, :, None]
    return jnp.where(
        digit == 0, value // 64, jnp.where(digit == 1, value % 64, 0)
    ).astype(jnp.bfloat16)


def read_labels(tails):
    line = tails[:, : 2 * (ROOM_PAD // WIDE), :].reshape(PLANES, ROOM_PAD // WIDE, 2, WIDE)
    line = jnp.transpose(line, (0, 2, 1, 3)).reshape(PLANES, 2, ROOM_PAD).astype(jnp.int32)
    pos = (line[:, 0, :] * 64 + line[:, 1, :] - 1)[:, :ROOM]
    over = jnp.max(tails[:, TAIL - 1, 0]).astype(jnp.int32)
    begin = jnp.arange(INNER) * OWNED
    ahead = jnp.sum(
        ((pos[:, None, :] >= 0) & (pos[:, None, :] < begin[None, :, None])).astype(jnp.int32), axis=2
    )
    first = jnp.minimum(ahead // CELL * CELL, ROOM - SPAN).astype(jnp.int32).reshape(-1)
    pos = jnp.pad(pos, ((0, 0), (0, CHOICE - ROOM)), constant_values=-1)
    return pos, first, over


def shards(query_rows, key_rows, value_rows, destination, doc_lengths, norm_gain):
    plane = lax.axis_index("z")
    inner = lax.axis_index("a")
    count = destination.shape[0]
    digits = jnp.concatenate([destination // WIDE, destination % WIDE]).astype(jnp.bfloat16)
    spare = jnp.pad(digits[None], ((0, CELL - 1), (0, 0)))
    key_rows_there = spread(split(key_rows, (), spare))
    digits = key_rows_there[:, count, :].astype(jnp.int32)
    places = (digits[:, :count] * WIDE + digits[:, count:]).reshape(-1)
    cell, strip, firsts, over = slotting(places, plane)
    value_rows_there = spread(split(value_rows, (cell, strip)))
    key_pieces = along(pack(firsts, cell, strip, key_rows_there))
    value_packed = pack(firsts, cell, strip, value_rows_there, label(places), over)
    query_rows_there = spread(split(query_rows, (value_rows_there,)))
    value_pieces = along(value_packed, tuple(key_pieces[1:]))
    query_packed = pack(firsts, cell, strip, query_rows_there, after=value_pieces[1:])
    query_pieces = along(query_packed)
    doc_lengths_then, _ = lax.optimization_barrier((doc_lengths, key_pieces[1]))
    value_pieces[0], _ = lax.optimization_barrier(
        (value_pieces[0], (query_pieces[1], query_pieces[7]))
    )
    pos, first, any_over = read_labels(jnp.stack([piece[ROOM:] for piece in value_pieces]))

    doc_ends = jnp.cumsum(doc_lengths_then)
    doc_begins = doc_ends - doc_lengths_then
    positions = plane * PLANE_ROWS + jnp.arange(PLANE_ROWS, dtype=jnp.int32)
    doc_start = jnp.max(
        jnp.where(doc_begins[None, :] <= positions[:, None], doc_begins[None, :], 0), axis=1
    )
    local_start = (doc_start - positions // OWNED * OWNED).astype(jnp.int32)
    last_local = local_start.reshape(INNER, OWNED)[:, OWNED - 1]
    block_at = jnp.arange(INNER)
    carries = jnp.all(
        (block_at[None, :] >= block_at[:, None]) | (last_local[None, :] < 0), axis=1
    ).astype(jnp.int32)

    choice, mask, use, keys, values, prior, end = states(
        first, last_local, pos, local_start[:, None], key_pieces, value_pieces
    )
    entry = lax.ppermute(end, "z", [(i, i + 1) for i in range(PLANES - 1)])
    gain = lax.dynamic_slice_in_dim(norm_gain.astype(jnp.float32), inner * WIDE, WIDE).reshape(1, WIDE)
    attended = attend(
        first, carries, choice, mask, use, gain, keys, values, prior, entry, query_pieces
    )
    back = lax.all_to_all(attended, "a", split_axis=0, concat_axis=0, tiled=True)
    return lax.cond(
        any_over > 0,
        lambda: direct(query_rows, key_rows, value_rows, destination, doc_lengths, norm_gain),
        lambda: join(back),
    )


def solution(mesh):
    fine = Mesh(mesh.devices.reshape(PLANES, INNER, mesh.shape["head"]), ("z", "a", "head"))
    every = ("z", "a", "head")
    in_specs = (P(every, None), P(every, None), P(every, None), P(every), P(), P("head"))
    return jax.shard_map(
        shards, mesh=fine, in_specs=in_specs, out_specs=P(SEQ, "head"), check_vma=False
    )
```
